256 devices in a mesh: seq: 64 (over y, x, z_hi), tp: 4 (over z_lo, core).
Axes of the slice: x: 4, y: 4, z: 8 (z_hi: 4, z_lo: 2; z = z_hi * 2 + z_lo), core: 2. Of those that a mesh axis runs over, the one named last changes fastest.
Arguments:
- query_proj: bfloat16 [65536, 4096], P('seq', 'tp'), may hold values from -6 to 6
- key_proj: bfloat16 [65536, 4096], P('seq', 'tp'), may hold values from -6 to 6
- value_proj: bfloat16 [65536, 4096], P('seq', 'tp'), may hold values from -6 to 6
- decay_rates: float32 [16, 4096], P(None, 'tp'), may hold values from 0 to 1, as said below
- residues: float32 [16, 4096], P(None, 'tp'), may hold values from -2 to 2
- skip_gain: float32 [4096], P('tp'), may hold values from -1 to 1
- out_weight: bfloat16 [4096, 4096], P('tp'), may hold values from -0.09375 to 0.09375
Outputs:
- mixed_out: bfloat16 [65536, 4096], P('seq', 'tp')
The draws below stay inside these ranges and needn't reach their ends.
Inputs may be any that keep to these rules, and one draw needn't show every extreme that they name: `decay_rates`: positive decay rates.
All inputs are finite; a program needn't handle non-finite values.
Results may differ from the reference program's by a relative error of at most 0.014.
Values may be sent and summed in bfloat16 or wider, within the bound.
No kernel may reach another device: no remote copies, remote signals or barrier semaphores. Data moves between devices by JAX's collectives and lax.ppermute only.
A program may use at most 192 MiB of HBM per device.

```python
import math
import jax
import jax.numpy as jnp
from jax import lax

CH = 4096
D_OUT = 4096
ORDER = 16
SUB = 32
TOK_DEV = 1024
SEQ_LEN = 65536
N_SEQ = 64
N_TP = 4


def draw_decay_rates(key, part):
    key = jax.random.fold_in(key, 11)
    first, second, third = jax.random.split(key, 3)
    slow_share = 0.5
    chooser = jax.random.uniform(first, (ORDER, CH), jnp.float32)
    broad = jnp.exp(jax.random.uniform(second, (ORDER, CH), jnp.float32, math.log(2.0 / SEQ_LEN), math.log(0.9)))
    slow = jnp.exp(jax.random.uniform(third, (ORDER, CH), jnp.float32, math.log(0.05 / SEQ_LEN), math.log(2.0 / SEQ_LEN)))
    return jnp.where(chooser < slow_share, slow, broad).astype(jnp.float32)


def shard_levels(key, dims, cuts, low, largest):
    def one(axis_at, shards_of):
        heights = jax.random.uniform(jax.random.fold_in(jax.random.fold_in(key, 6), axis_at), (shards_of,), jnp.float32, low / len(cuts), largest / len(cuts))
        return jnp.repeat(jnp.exp(heights), dims[axis_at] // shards_of).reshape((-1,) + (1,) * (len(dims) - axis_at - 1))

    level = one(*cuts[0])
    for cut in cuts[1:]:
        level = level * one(*cut)
    return level


def scatter_about(key, shape, spread, limit, cuts=(), held_as=jnp.bfloat16):
    loudness = shard_levels(key, shape, cuts, -0.22, 0.18) if cuts else 1.0
    values = jax.random.normal(key, shape, jnp.float32) * spread * loudness
    return jnp.minimum(jnp.maximum(values, -limit), limit).astype(held_as)


def setup_inputs(seed: int = 0) -> dict:
    streams_of = jax.random.split(jax.random.key(seed), 8)
    query_proj = scatter_about(streams_of[0], (SEQ_LEN, CH), 1.0, 6.0, ((0, 64), (1, 4)))
    key_proj = scatter_about(streams_of[1], (SEQ_LEN, CH), 1.0, 6.0, ((0, 64), (1, 4)))
    value_proj = scatter_about(streams_of[2], (SEQ_LEN, CH), 1.0, 6.0, ((0, 64), (1, 4)))
    decay_rates = draw_decay_rates(jax.random.fold_in(streams_of[7], 71), 0)
    residues = scatter_about(streams_of[4], (ORDER, CH), 0.35, 2.0, ((1, 4),), jnp.float32)
    skip_gain = jnp.clip(jax.random.uniform(streams_of[5], (CH,), jnp.float32, -1.0, 1.0) * shard_levels(streams_of[5], (CH,), ((0, 4),), -0.4, 0.0), -1.0, 1.0)
    out_weight = scatter_about(streams_of[6], (CH, D_OUT), CH ** -0.5, 0.09375, ((0, 4),))
    return dict(query_proj=query_proj, key_proj=key_proj, value_proj=value_proj, decay_rates=decay_rates, residues=residues, skip_gain=skip_gain, out_weight=out_weight)


def modal_tables(decay_rates, residues, sub_len):
    positions = jnp.arange(sub_len, dtype=jnp.float32)
    powers = jnp.exp(-decay_rates[None] * positions[:, None, None])
    weights_modal = residues * jnp.sqrt(decay_rates)
    return (positions, powers, weights_modal)

def block_convolve(inputs, decay_rates, residues, start_state, sub_len):
    tok_rows, chan_count = inputs.shape
    sub_count = tok_rows // sub_len
    positions, powers, weights_modal = modal_tables(decay_rates, residues, sub_len)
    kernel_taps = jnp.einsum('tnc,nc->tc', powers, weights_modal, precision=lax.Precision.HIGHEST)
    distance = positions[:, None] - positions[None, :]
    onehot = (distance[:, :, None] == positions[None, None, :]).astype(jnp.float32)
    toeplitz = jnp.einsum('tsd,dc->tsc', onehot, kernel_taps, precision=lax.Precision.HIGHEST)
    pieces = inputs.reshape(sub_count, sub_len, chan_count)
    inside = jnp.einsum('tsc,msc->mtc', toeplitz, pieces, precision=lax.Precision.HIGHEST)
    end_states = jnp.einsum('snc,msc->mnc', powers[::-1], pieces, precision=lax.Precision.HIGHEST)
    step_decay = jnp.exp(-decay_rates * sub_len)

    def advance(carry_state, block_end):
        return (step_decay * carry_state + block_end, carry_state)
    final_state, before = lax.scan(advance, start_state, end_states)
    reach_table = powers * jnp.exp(-decay_rates)[None] * weights_modal[None]
    carried = jnp.einsum('tnc,mnc->mtc', reach_table, before, precision=lax.Precision.HIGHEST)
    return ((inside + carried).reshape(tok_rows, chan_count), final_state)

def reference(query_proj, key_proj, value_proj, decay_rates, residues, skip_gain, out_weight):
    group_width = CH // N_TP
    stacked = (query_proj.reshape(N_SEQ, TOK_DEV, CH), key_proj.reshape(N_SEQ, TOK_DEV, CH), value_proj.reshape(N_SEQ, TOK_DEV, CH))

    def one_block(carry_state, blocks):
        query_block, key_block, value_block = blocks
        inputs = key_block.astype(jnp.float32) * value_block.astype(jnp.float32)
        convolved, final_state = block_convolve(inputs, decay_rates, residues, carry_state, SUB)
        gated = (query_block.astype(jnp.float32) * (convolved + skip_gain[None] * inputs)).astype(jnp.bfloat16)
        summed = jnp.zeros((TOK_DEV, D_OUT), jnp.float32)
        for group in range(N_TP):
            partial_value = jnp.dot(gated[:, group * group_width:(group + 1) * group_width], out_weight[group * group_width:(group + 1) * group_width], preferred_element_type=jnp.float32)
            partial_value = lax.optimization_barrier(partial_value.astype(jnp.bfloat16)).astype(jnp.float32)
            summed = summed + partial_value
        return (final_state, summed.astype(jnp.bfloat16))
    start_state = jnp.zeros((ORDER, CH), jnp.float32)
    unused, outputs = lax.scan(one_block, start_state, stacked)
    return outputs.reshape(SEQ_LEN, D_OUT)
```

```python
import functools

import jax
import jax.numpy as jnp
from jax import lax
from jax.experimental import pallas as pl
from jax.experimental.pallas import tpu as pltpu
from jax.sharding import PartitionSpec as P

SEG = 8
LANES = 128
SPANS = (16, 16, 32, 32, 32)
VMEM_LIMIT = 32 * 2**20
VMEM_ALL = 60 * 2**20
SIBLING = [(0, 1), (1, 0), (2, 3), (3, 2)]
PARTNER = [(0, 2), (2, 0), (1, 3), (3, 1)]
ANY = pl.BlockSpec(memory_space=pl.ANY)


def cost(flops, moved):
    return pl.CostEstimate(flops=1, bytes_accessed=1, transcendentals=0)


def end_kernel(seg_len, k_ref, v_ref, lam_ref, last_ref, before_ref, sent_ref, x_ref):
    order = lam_ref.shape[0]
    pitch = seg_len + 1
    for group in range(k_ref.shape[1] // LANES):
        cols = slice(group * LANES, (group + 1) * LANES)
        for seg in range(SEG):
            rows = pl.ds(seg * seg_len, seg_len)
            x = k_ref[rows, cols].astype(jnp.float32) * v_ref[rows, cols].astype(jnp.float32)
            x_ref[pl.ds(seg * pitch, seg_len), :] = x
        lam = [jnp.broadcast_to(lam_ref[n : n + 1, cols], (SEG, LANES)) for n in range(order)]
        decay = [jnp.exp(-rate) for rate in lam]

        def body(it, state):
            for u in range(16):
                x = x_ref[pl.ds(it * 16 + u, SEG, stride=pitch), :]
                state = tuple(h * d + x for h, d in zip(state, decay))
            return state

        zero = jnp.zeros((SEG, LANES), jnp.float32)
        state = lax.fori_loop(0, seg_len // 16, body, (zero,) * order)
        row = lax.broadcasted_iota(jnp.int32, (SEG, LANES), 0)
        for n in range(order):
            run = state[n]
            for step in (1, 2, 4):
                hop = jnp.exp(lam[n] * (-float(seg_len * step)))
                run = run + jnp.where(row >= step, hop * pltpu.roll(run, step, 0), 0.0)
            last_ref[n : n + 1, cols] = run[SEG - 1 : SEG]
            sent_ref[n : n + 1, cols] = run[SEG - 1 : SEG].astype(jnp.bfloat16)
            before_ref[n * SEG : (n + 1) * SEG, cols] = jnp.where(
                row >= 1, pltpu.roll(run, 1, 0), 0.0
            )


def end_states(key, value, rates, width=256):
    tok, ch = key.shape
    order = rates.shape[0]
    seg_len = tok // SEG
    cut = lambda rows: pl.BlockSpec((rows, width), lambda j: (0, j))
    return pl.pallas_call(
        functools.partial(end_kernel, seg_len),
        grid=(ch // width,),
        in_specs=[cut(tok), cut(tok), cut(order)],
        out_specs=[cut(order), cut(order * SEG), cut(order)],
        out_shape=[
            jax.ShapeDtypeStruct((order, ch), jnp.float32),
            jax.ShapeDtypeStruct((order * SEG, ch), jnp.float32),
            jax.ShapeDtypeStruct((order, ch), jnp.bfloat16),
        ],
        scratch_shapes=[pltpu.VMEM((SEG * (seg_len + 1), LANES), jnp.float32)],
        compiler_params=pltpu.CompilerParams(vmem_limit_bytes=VMEM_ALL),
        cost_estimate=cost(2 * tok * ch * order, 4 * tok * ch),
        name="end_states",
    )(key, value, rates)


def gate_kernel(first, late, seg_len, q_ref, k_ref, v_ref, lam_ref, res_ref, skip_ref, state_ref, *rest):
    g_ref, next_ref, x_ref, y_ref = rest[-4:]
    if first:
        inc_ref = rest[0]
    order = lam_ref.shape[0]
    span = q_ref.shape[1]
    pitch = span + 1
    for group in range(q_ref.shape[2] // LANES):
        cols = slice(group * LANES, (group + 1) * LANES)
        for seg in range(SEG):
            x = k_ref[seg, :, cols].astype(jnp.float32) * v_ref[seg, :, cols].astype(jnp.float32)
            x_ref[pl.ds(seg * pitch, span), :] = x
        lam = [jnp.broadcast_to(lam_ref[n : n + 1, cols], (SEG, LANES)) for n in range(order)]
        decay = [jnp.exp(-rate) for rate in lam]
        weight = [res_ref[n : n + 1, cols] * jnp.sqrt(lam[n]) for n in range(order)]
        state = [state_ref[n * SEG : (n + 1) * SEG, cols] for n in range(order)]
        if first:
            row = lax.broadcasted_iota(jnp.int32, (SEG, LANES), 0).astype(jnp.float32)
            reach = row * (-float(seg_len)) - float(late)
            state = [
                h + jnp.exp(lam[n] * reach) * inc_ref[n : n + 1, cols]
                for n, h in enumerate(state)
            ]

        def body(it, state):
            for u in range(16):
                where = pl.ds(it * 16 + u, SEG, stride=pitch)
                x = x_ref[where, :]
                state = tuple(h * d + x for h, d in zip(state, decay))
                terms = [w * h for w, h in zip(weight, state)]
                while len(terms) > 1:
                    terms = [a + b for a, b in zip(terms[::2], terms[1::2])]
                y_ref[where, :] = terms[0]
            return state

        if span == 16:
            state = body(0, tuple(state))
        else:
            state = lax.fori_loop(0, span // 16, body, tuple(state))
        for n in range(order):
            next_ref[n * SEG : (n + 1) * SEG, cols] = state[n]
        skip = skip_ref[:, cols]
        for seg in range(SEG):
            rows = pl.ds(seg * pitch, span)
            gate = q_ref[seg, :, cols].astype(jnp.float32) * (y_ref[rows, :] + skip * x_ref[rows, :])
            g_ref[seg, :, cols] = gate.astype(jnp.bfloat16)


def gate_chunk(
    query, key, value, rates, residues, skip, state, incoming, after, at, span, width=512
):
    seg, seg_len, ch = query.shape
    order = rates.shape[0]
    first = incoming is not None
    part = pl.BlockSpec((seg, span, width), lambda j: (0, at // span, j))
    cut = lambda rows: pl.BlockSpec((rows, width), lambda j: (0, j))
    operands = [query, key, value, rates, residues, skip, state]
    in_specs = [part, part, part, cut(order), cut(order), cut(1), cut(order * seg)]
    if first:
        operands.append(incoming)
        in_specs.append(cut(order))
    operands.extend(after)
    in_specs.extend([ANY] * len(after))
    rows = seg * span
    gated, state = pl.pallas_call(
        functools.partial(gate_kernel, first, at, seg_len),
        grid=(ch // width,),
        in_specs=in_specs,
        out_specs=[pl.BlockSpec((seg, span, width), lambda j: (0, 0, j)), cut(order * seg)],
        out_shape=[
            jax.ShapeDtypeStruct((seg, span, ch), jnp.bfloat16),
            jax.ShapeDtypeStruct((order * seg, ch), jnp.float32),
        ],
        scratch_shapes=[pltpu.VMEM((seg * (span + 1), LANES), jnp.float32)] * 2,
        compiler_params=pltpu.CompilerParams(vmem_limit_bytes=VMEM_LIMIT),
        cost_estimate=cost(4 * rows * ch * order, 8 * rows * ch + 8 * order * seg * ch),
        name="gate_chunk",
    )(*operands)
    return gated.reshape(rows, ch), state


def columns_kernel(at_ref, w_ref, wo_ref, out_ref):
    depth = w_ref.shape[0]
    out_ref[:depth] = w_ref[...]
    out_ref[depth:] = wo_ref[...]


def chip_columns(block, weight, weight_other, width=512):
    ch = weight.shape[0]
    per = ch // width
    part = pl.BlockSpec((ch, width), lambda j, at: (0, at[0] * per + j))
    return pl.pallas_call(
        columns_kernel,
        grid_spec=pltpu.PrefetchScalarGridSpec(
            num_scalar_prefetch=1,
            grid=(per,),
            in_specs=[part, part],
            out_specs=pl.BlockSpec((2 * ch, width), lambda j, at: (0, j)),
        ),
        out_shape=jax.ShapeDtypeStruct((2 * ch, ch), weight.dtype),
        compiler_params=pltpu.CompilerParams(vmem_limit_bytes=VMEM_LIMIT),
        cost_estimate=cost(0, 8 * ch * ch),
        name="chip_columns",
    )(block, weight, weight_other)


def product(mine, other, weight):
    depth = weight.shape[0] // 2
    total = jnp.dot(mine, weight[:depth], preferred_element_type=jnp.float32)
    return total + jnp.dot(other, weight[depth:], preferred_element_type=jnp.float32)


def share_kernel(mine_ref, other_ref, w_ref, *rest):
    out_ref = rest[-1]
    out_ref[...] = product(mine_ref[...], other_ref[...], w_ref[...]).astype(out_ref.dtype)


def share_chunk(mine, other, weight, after, width=512):
    rows, ch = mine.shape
    whole = pl.BlockSpec((rows, ch), lambda j: (0, 0))
    return pl.pallas_call(
        share_kernel,
        grid=(ch // width,),
        in_specs=[whole, whole, pl.BlockSpec((2 * ch, width), lambda j: (0, j))] + [ANY] * len(after),
        out_specs=pl.BlockSpec((rows, width), lambda j: (0, j)),
        out_shape=jax.ShapeDtypeStruct((rows, ch), jnp.bfloat16),
        compiler_params=pltpu.CompilerParams(vmem_limit_bytes=VMEM_LIMIT),
        cost_estimate=cost(4 * rows * ch * ch, 4 * ch * ch + 6 * rows * ch),
        name="share_chunk",
    )(mine, other, weight, *after)


def own_kernel(count, w_ref, *rest):
    parts, outs = rest[: 2 * count], rest[-count:]
    for i in range(count):
        outs[i][...] = product(parts[2 * i][...], parts[2 * i + 1][...], w_ref[...])


def own_shares(weight, pairs, after, width=256):
    ch = weight.shape[1]
    rows = [mine.shape[0] for mine, _ in pairs]
    whole = [pl.BlockSpec((r, ch), lambda j: (0, 0)) for r in rows for _ in range(2)]
    return pl.pallas_call(
        functools.partial(own_kernel, len(pairs)),
        grid=(ch // width,),
        in_specs=[pl.BlockSpec((2 * ch, width), lambda j: (0, j)), *whole] + [ANY] * len(after),
        out_specs=[pl.BlockSpec((r, width), lambda j: (0, j)) for r in rows],
        out_shape=[jax.ShapeDtypeStruct((r, ch), jnp.float32) for r in rows],
        compiler_params=pltpu.CompilerParams(vmem_limit_bytes=VMEM_LIMIT),
        cost_estimate=cost(4 * sum(rows) * ch * ch, 4 * ch * ch + 8 * sum(rows) * ch),
        name="own_shares",
    )(weight, *[part for pair in pairs for part in pair], *after)


def finish_kernel(mine_ref, far_ref, *rest):
    out_ref = rest[-1]
    total = mine_ref[...] + far_ref[...].astype(jnp.float32)
    out_ref[...] = total.astype(out_ref.dtype).reshape(out_ref.shape)


def finish_chunk(mine, far, out, at, span, seg_len, width=512):
    rows, ch = mine.shape
    seg = rows // span
    cut = pl.BlockSpec((rows, width), lambda j: (0, j))
    operands, in_specs, aliases = [mine, far], [cut, cut], {}
    if out is not None:
        operands.append(out)
        in_specs.append(ANY)
        aliases = {2: 0}
    return pl.pallas_call(
        finish_kernel,
        grid=(ch // width,),
        in_specs=in_specs,
        out_specs=pl.BlockSpec((seg, span, width), lambda j: (0, at // span, j)),
        out_shape=jax.ShapeDtypeStruct((seg, seg_len, ch), jnp.bfloat16),
        input_output_aliases=aliases,
        compiler_params=pltpu.CompilerParams(vmem_limit_bytes=VMEM_LIMIT),
        cost_estimate=cost(rows * ch, 8 * rows * ch),
        name="finish_chunk",
    )(*operands)


def in_hbm(array):
    return pltpu.with_memory_space_constraint(array, pltpu.HBM)


def shifted(sizes, dim, hop, wrap):
    pairs = []
    total = 1
    for size in sizes:
        total *= size
    inner = 1
    for size in sizes[dim + 1 :]:
        inner *= size
    size = sizes[dim]
    for index in range(total):
        place = index // inner % size
        goal = place + hop
        if goal >= size and not wrap:
            continue
        pairs.append((index, index + (goal % size - place) * inner))
    return pairs


def carried_in(state, sent, rates, length, sizes, held):
    mine = lax.axis_index("seq")
    incoming = None
    reach = float(length)
    levels = []
    for dim in reversed(range(len(sizes))):
        size = sizes[dim]
        place = mine % size
        mine = mine // size
        wrap = dim > 0
        if sent is None:
            sent = state.astype(jnp.bfloat16)
        if dim == 0:
            sent, held = lax.optimization_barrier((sent, held))
        got = [
            lax.ppermute(sent, "seq", shifted(sizes, dim, hop, wrap)).astype(jnp.float32)
            for hop in range(1, size)
        ]
        drop = lambda blocks: jnp.exp(rates * (-reach * blocks))
        prefix = sum(
            jnp.where(hop <= place, drop(float(hop - 1)), 0.0) * part
            for hop, part in enumerate(got, 1)
        )
        sent = None
        levels.append((prefix, drop(place.astype(jnp.float32))))
        if dim > 0:
            state = state * drop((size - 1 - place).astype(jnp.float32)) + sum(
                drop((size - 1 - (place - hop) % size).astype(jnp.float32)) * part
                for hop, part in enumerate(got, 1)
            )
        reach = reach * size
    incoming = levels[-1][0]
    for prefix, fade in reversed(levels[:-1]):
        incoming = prefix + fade * incoming
    return incoming, held


def on_device(sizes, query, key, value, rates, residues, skip_gain, weight):
    tok, ch = query.shape
    seg_len = tok // SEG
    here = lax.axis_index("tp")
    chip, core = here // 2, here % 2
    weight_other = in_hbm(lax.ppermute(weight, "tp", SIBLING))
    weight = in_hbm(weight)
    last, before, sent = end_states(key, value, rates)
    weight_far, weight_near = (
        chip_columns(jnp.stack([block]).astype(jnp.int32), weight, weight_other)
        for block in (2 * (1 - chip) + core, here)
    )
    incoming, weight_far = carried_in(last, sent, rates, tok, sizes, weight_far)
    view = lambda part: part.reshape(SEG, seg_len, ch)
    query, key, value = (in_hbm(view(part)) for part in (query, key, value))
    state, extra = before, incoming
    at = 0
    parts, shares, came = [], [], []
    for i, span in enumerate(SPANS):
        after = ([shares[i - 2], came[max(i - 3, 0)]]) if i >= 2 else []
        gated, state = gate_chunk(
            query, key, value, rates, residues, skip_gain[None],
            state, extra, after, at, span,
        )
        extra = None
        other = lax.ppermute(gated, "tp", SIBLING)
        shares.append(share_chunk(gated, other, weight_far, shares[-1:]))
        came.append(lax.ppermute(shares[-1], "tp", PARTNER))
        parts.append((at, span, gated, other))
        at += span
    own = own_shares(weight_near, [part[2:4] for part in parts], [shares[-1], came[-3]])
    out = None
    for mine, far_share, (at, span, _, _) in zip(own, came, parts):
        out = finish_chunk(mine, far_share, out, at, span, seg_len)
    return out.reshape(tok, ch)


def solution(mesh):
    placed = (
        P("seq", "tp"),
        P("seq", "tp"),
        P("seq", "tp"),
        P(None, "tp"),
        P(None, "tp"),
        P("tp"),
        P("tp", None),
    )
    return jax.shard_map(
        functools.partial(on_device, (4, 4, 4)),
        mesh=mesh,
        in_specs=placed,
        out_specs=P("seq", "tp"),
        check_vma=False,
    )
```

```python
import functools

import jax
import jax.numpy as jnp
from jax import lax
from jax.experimental import pallas as pl
from jax.experimental.pallas import tpu as pltpu
from jax.sharding import PartitionSpec as P

SEG = 8
LANES = 128
SPANS = (32, 32, 32, 32)
PIECE = 64
VMEM_LIMIT = 32 * 2**20
SIBLING = [(0, 1), (1, 0), (2, 3), (3, 2)]
PARTNER = [(0, 2), (2, 0), (1, 3), (3, 1)]
ANY = pl.BlockSpec(memory_space=pl.ANY)


def cost(flops, moved):
    return pl.CostEstimate(flops=1, bytes_accessed=1, transcendentals=0)


def end_kernel(seg_len, k_ref, v_ref, lam_ref, last_ref, before_ref, sent_ref, x_ref):
    order = lam_ref.shape[0]
    pitch = seg_len + 1
    for group in range(k_ref.shape[1] // LANES):
        cols = slice(group * LANES, (group + 1) * LANES)
        for seg in range(SEG):
            rows = pl.ds(seg * seg_len, seg_len)
            x = k_ref[rows, cols].astype(jnp.float32) * v_ref[rows, cols].astype(jnp.float32)
            x_ref[pl.ds(seg * pitch, seg_len), :] = x
        lam = [jnp.broadcast_to(lam_ref[n : n + 1, cols], (SEG, LANES)) for n in range(order)]
        decay = [jnp.exp(-rate) for rate in lam]

        def body(it, state):
            for u in range(16):
                x = x_ref[pl.ds(it * 16 + u, SEG, stride=pitch), :]
                state = tuple(h * d + x for h, d in zip(state, decay))
            return state

        zero = jnp.zeros((SEG, LANES), jnp.float32)
        state = lax.fori_loop(0, seg_len // 16, body, (zero,) * order)
        row = lax.broadcasted_iota(jnp.int32, (SEG, LANES), 0)
        for n in range(order):
            run = state[n]
            for step in (1, 2, 4):
                hop = jnp.exp(lam[n] * (-float(seg_len * step)))
                run = run + jnp.where(row >= step, hop * pltpu.roll(run, step, 0), 0.0)
            last_ref[n : n + 1, cols] = run[SEG - 1 : SEG]
            sent_ref[n : n + 1, cols] = run[SEG - 1 : SEG].astype(jnp.bfloat16)
            before_ref[n * SEG : (n + 1) * SEG, cols] = jnp.where(
                row >= 1, pltpu.roll(run, 1, 0), 0.0
            )


def end_states(key, value, rates, width=256):
    tok, ch = key.shape
    order = rates.shape[0]
    seg_len = tok // SEG
    cut = lambda rows: pl.BlockSpec((rows, width), lambda j: (0, j))
    return pl.pallas_call(
        functools.partial(end_kernel, seg_len),
        grid=(ch // width,),
        in_specs=[cut(tok), cut(tok), cut(order)],
        out_specs=[cut(order), cut(order * SEG), cut(order)],
        out_shape=[
            jax.ShapeDtypeStruct((order, ch), jnp.float32),
            jax.ShapeDtypeStruct((order * SEG, ch), jnp.float32),
            jax.ShapeDtypeStruct((order, ch), jnp.bfloat16),
        ],
        scratch_shapes=[pltpu.VMEM((SEG * (seg_len + 1), LANES), jnp.float32)],
        compiler_params=pltpu.CompilerParams(vmem_limit_bytes=VMEM_LIMIT),
        cost_estimate=cost(2 * tok * ch * order, 4 * tok * ch),
        name="end_states",
    )(key, value, rates)


def gate_kernel(first, late, seg_len, q_ref, k_ref, v_ref, lam_ref, res_ref, skip_ref, state_ref, *rest):
    next_ref, x_ref, y_ref = rest[-3:]
    if first:
        inc_ref = rest[0]
    order = lam_ref.shape[0]
    span = q_ref.shape[1]
    held = PIECE // span
    g_refs = rest[-3 - SEG // held : -3]
    pitch = span + 1
    for group in range(q_ref.shape[2] // LANES):
        cols = slice(group * LANES, (group + 1) * LANES)
        for seg in range(SEG):
            x = k_ref[seg, :, cols].astype(jnp.float32) * v_ref[seg, :, cols].astype(jnp.float32)
            x_ref[pl.ds(seg * pitch, span), :] = x
        lam = [jnp.broadcast_to(lam_ref[n : n + 1, cols], (SEG, LANES)) for n in range(order)]
        decay = [jnp.exp(-rate) for rate in lam]
        weight = [res_ref[n : n + 1, cols] * jnp.sqrt(lam[n]) for n in range(order)]
        state = [state_ref[n * SEG : (n + 1) * SEG, cols] for n in range(order)]
        if first:
            row = lax.broadcasted_iota(jnp.int32, (SEG, LANES), 0).astype(jnp.float32)
            reach = row * (-float(seg_len)) - float(late)
            state = [
                h + jnp.exp(lam[n] * reach) * inc_ref[n : n + 1, cols]
                for n, h in enumerate(state)
            ]

        def body(it, state):
            for u in range(16):
                where = pl.ds(it * 16 + u, SEG, stride=pitch)
                x = x_ref[where, :]
                state = tuple(h * d + x for h, d in zip(state, decay))
                terms = [w * h for w, h in zip(weight, state)]
                while len(terms) > 1:
                    terms = [a + b for a, b in zip(terms[::2], terms[1::2])]
                y_ref[where, :] = terms[0]
            return state

        if span == 16:
            state = body(0, tuple(state))
        else:
            state = lax.fori_loop(0, span // 16, body, tuple(state))
        for n in range(order):
            next_ref[n * SEG : (n + 1) * SEG, cols] = state[n]
        skip = skip_ref[:, cols]
        for seg in range(SEG):
            rows = pl.ds(seg * pitch, span)
            gate = q_ref[seg, :, cols].astype(jnp.float32) * (y_ref[rows, :] + skip * x_ref[rows, :])
            g_refs[seg // held][seg % held, :, cols] = gate.astype(jnp.bfloat16)


def gate_chunk(
    query, key, value, rates, residues, skip, state, incoming, after, at, span, width=None
):
    seg, seg_len, ch = query.shape
    order = rates.shape[0]
    first = incoming is not None
    width = width or (512 if span <= 16 else 256)
    part = pl.BlockSpec((seg, span, width), lambda j: (0, at // span, j))
    cut = lambda rows: pl.BlockSpec((rows, width), lambda j: (0, j))
    operands = [query, key, value, rates, residues, skip, state]
    in_specs = [part, part, part, cut(order), cut(order), cut(1), cut(order * seg)]
    if first:
        operands.append(incoming)
        in_specs.append(cut(order))
    operands.extend(after)
    in_specs.extend([ANY] * len(after))
    rows = seg * span
    held = PIECE // span
    count = seg // held
    *gated, state = pl.pallas_call(
        functools.partial(gate_kernel, first, at, seg_len),
        grid=(ch // width,),
        in_specs=in_specs,
        out_specs=[pl.BlockSpec((held, span, width), lambda j: (0, 0, j))] * count
        + [cut(order * seg)],
        out_shape=[jax.ShapeDtypeStruct((held, span, ch), jnp.bfloat16)] * count
        + [
            jax.ShapeDtypeStruct((order * seg, ch), jnp.float32),
        ],
        scratch_shapes=[pltpu.VMEM((seg * (span + 1), LANES), jnp.float32)] * 2,
        compiler_params=pltpu.CompilerParams(vmem_limit_bytes=VMEM_LIMIT),
        cost_estimate=cost(4 * rows * ch * order, 8 * rows * ch + 8 * order * seg * ch),
        name="gate_chunk",
    )(*operands)
    return [piece.reshape(PIECE, ch) for piece in gated], state


def columns_kernel(at_ref, w_ref, wo_ref, out_ref, mark_ref):
    mark_ref[...] = jnp.zeros_like(mark_ref)
    depth = w_ref.shape[0]
    out_ref[:depth] = w_ref[...]
    out_ref[depth:] = wo_ref[...]


def chip_columns(block, weight, weight_other, order, width=512):
    ch = weight.shape[0]
    per = ch // width
    part = pl.BlockSpec((ch, width), lambda j, at: (0, at[0] * per + j))
    return pl.pallas_call(
        columns_kernel,
        grid_spec=pltpu.PrefetchScalarGridSpec(
            num_scalar_prefetch=1,
            grid=(per,),
            in_specs=[part, part],
            out_specs=[
                pl.BlockSpec((2 * ch, width), lambda j, at: (0, j)),
                pl.BlockSpec((order, width), lambda j, at: (0, j)),
            ],
        ),
        out_shape=[
            pltpu.HBM((2 * ch, ch), weight.dtype),
            jax.ShapeDtypeStruct((order, ch), jnp.float32),
        ],
        compiler_params=pltpu.CompilerParams(vmem_limit_bytes=VMEM_LIMIT),
        cost_estimate=cost(0, 8 * ch * ch),
        name="chip_columns",
    )(block, weight, weight_other)


def gathered(pieces):
    return jnp.concatenate([piece[...] for piece in pieces], axis=0)


def product(mine, other, weight, weight_other):
    total = jnp.dot(gathered(mine), weight, preferred_element_type=jnp.float32)
    return total + jnp.dot(gathered(other), weight_other, preferred_element_type=jnp.float32)


def share_kernel(count, w_ref, *rest):
    out_ref = rest[-1]
    depth = w_ref.shape[0] // 2
    total = product(rest[:count], rest[count : 2 * count], w_ref[:depth], w_ref[depth:])
    out_ref[...] = total.astype(out_ref.dtype)


def share_chunk(mine, other, weight, after, width=512):
    count = len(mine)
    ch = weight.shape[1]
    rows = count * PIECE
    return pl.pallas_call(
        functools.partial(share_kernel, count),
        grid=(ch // width,),
        in_specs=[pl.BlockSpec((2 * ch, width), lambda j: (0, j))]
        + [pl.BlockSpec((PIECE, ch), lambda j: (0, 0))] * (2 * count)
        + [ANY] * len(after),
        out_specs=pl.BlockSpec((rows, width), lambda j: (0, j)),
        out_shape=jax.ShapeDtypeStruct((rows, ch), jnp.bfloat16),
        compiler_params=pltpu.CompilerParams(vmem_limit_bytes=VMEM_LIMIT),
        cost_estimate=cost(4 * rows * ch * ch, 4 * ch * ch + 6 * rows * ch),
        name="share_chunk",
    )(weight, *mine, *other, *after)


def own_kernel(counts, at_ref, w_ref, wo_ref, *rest):
    outs = rest[-len(counts) :]
    at = 0
    for count, out_ref in zip(counts, outs):
        out_ref[...] = product(
            rest[at : at + count], rest[at + count : at + 2 * count], w_ref[...], wo_ref[...]
        )
        at += 2 * count


def own_shares(block, weight, weight_other, pairs, after, width=256):
    ch = weight.shape[0]
    per = ch // width
    counts = [len(mine) for mine, _ in pairs]
    pieces = [piece for mine, other in pairs for piece in [*mine, *other]]
    rows = [count * PIECE for count in counts]
    columns = pl.BlockSpec((ch, width), lambda j, at: (0, at[0] * per + j))
    return pl.pallas_call(
        functools.partial(own_kernel, counts),
        grid_spec=pltpu.PrefetchScalarGridSpec(
            num_scalar_prefetch=1,
            grid=(per,),
            in_specs=[columns, columns]
            + [pl.BlockSpec((PIECE, ch), lambda j, at: (0, 0))] * len(pieces)
            + [ANY] * len(after),
            out_specs=[pl.BlockSpec((r, width), lambda j, at: (0, j)) for r in rows],
        ),
        out_shape=[jax.ShapeDtypeStruct((r, ch), jnp.float32) for r in rows],
        compiler_params=pltpu.CompilerParams(vmem_limit_bytes=VMEM_LIMIT),
        cost_estimate=cost(4 * sum(rows) * ch * ch, 4 * ch * ch + 8 * sum(rows) * ch),
        name="own_shares",
    )(block, weight, weight_other, *pieces, *after)


def finish_kernel(mine_ref, far_ref, *rest):
    out_ref = rest[-1]
    total = mine_ref[...] + far_ref[...].astype(jnp.float32)
    out_ref[...] = total.astype(out_ref.dtype).reshape(out_ref.shape)


def finish_chunk(mine, far, out, at, span, seg_len, width=512):
    rows, ch = mine.shape
    seg = rows // span
    cut = pl.BlockSpec((rows, width), lambda j: (0, j))
    operands, in_specs, aliases = [mine, far], [cut, cut], {}
    if out is not None:
        operands.append(out)
        in_specs.append(ANY)
        aliases = {2: 0}
    return pl.pallas_call(
        finish_kernel,
        grid=(ch // width,),
        in_specs=in_specs,
        out_specs=pl.BlockSpec((seg, span, width), lambda j: (0, at // span, j)),
        out_shape=jax.ShapeDtypeStruct((seg, seg_len, ch), jnp.bfloat16),
        input_output_aliases=aliases,
        compiler_params=pltpu.CompilerParams(vmem_limit_bytes=VMEM_LIMIT),
        cost_estimate=cost(rows * ch, 8 * rows * ch),
        name="finish_chunk",
    )(*operands)


def in_hbm(array):
    return pltpu.with_memory_space_constraint(array, pltpu.HBM)


def shifted(sizes, dim, hop, wrap):
    pairs = []
    total = 1
    for size in sizes:
        total *= size
    inner = 1
    for size in sizes[dim + 1 :]:
        inner *= size
    size = sizes[dim]
    for index in range(total):
        place = index // inner % size
        goal = place + hop
        if goal >= size and not wrap:
            continue
        pairs.append((index, index + (goal % size - place) * inner))
    return pairs


def carried_in(state, sent, rates, length, sizes, marks):
    mine = lax.axis_index("seq")
    fade = jnp.exp(rates * (-float(length)))
    levels = []
    for dim in reversed(range(len(sizes))):
        size = sizes[dim]
        place = mine % size
        mine = mine // size
        got = [
            lax.ppermute(sent, "seq", shifted(sizes, dim, hop, True))
            for hop in range(1, size)
        ]
        got = [part.astype(jnp.float32) for part in got]
        if dim in marks:
            got = [part + marks[dim] for part in got]
        powers = [jnp.ones_like(fade), fade]
        while len(powers) <= size:
            powers.append(powers[-1] * fade)

        def power(exponent):
            return sum(jnp.where(exponent == i, powers[i], 0.0) for i in range(size))

        prefix = sum(
            jnp.where(hop <= place, powers[hop - 1], 0.0) * part
            for hop, part in enumerate(got, 1)
        )
        levels.append((prefix, power(place)))
        if dim > 0:
            state = state * power(size - 1 - place) + sum(
                power(size - 1 - (place - hop) % size) * part for hop, part in enumerate(got, 1)
            )
            sent = state.astype(jnp.bfloat16)
        fade = powers[size]
    incoming = levels[-1][0]
    for prefix, drop in reversed(levels[:-1]):
        incoming = prefix + drop * incoming
    return incoming


def on_device(sizes, query, key, value, rates, residues, skip_gain, weight):
    tok, ch = query.shape
    seg_len = tok // SEG
    here = lax.axis_index("tp")
    chip, core = here // 2, here % 2
    weight_other = in_hbm(lax.ppermute(weight, "tp", SIBLING))
    weight = in_hbm(weight)
    last, before, sent = end_states(in_hbm(key), in_hbm(value), rates)
    block = jnp.stack([2 * (1 - chip) + core]).astype(jnp.int32)
    weight_far, far_mark = chip_columns(block, weight, weight_other, rates.shape[0])
    incoming = carried_in(last, sent, rates, tok, sizes, {1: far_mark})
    view = lambda part: part.reshape(SEG, seg_len, ch)
    query, key, value = (in_hbm(view(part)) for part in (query, key, value))
    state, extra = before, incoming
    at = 0
    parts, shares, came = [], [], []
    gates, others = [], []

    def gate(i, after):
        nonlocal state, extra, at
        gated, state = gate_chunk(
            query, key, value, rates, residues, skip_gain[None],
            state, extra, after, at, SPANS[i],
        )
        extra = None
        gates.append(gated)
        others.append([lax.ppermute(piece, "tp", SIBLING) for piece in gated])
        parts.append((at, SPANS[i]))
        at += SPANS[i]

    def share(i, after):
        shares.append(share_chunk(gates[i], others[i], weight_far, after))
        came.append(lax.ppermute(shares[-1], "tp", PARTNER))

    gate(0, [])
    share(0, [])
    gate(1, [shares[0]])
    share(1, [shares[0]])
    gate(2, [shares[1]])
    gate(3, [came[0]])
    share(2, [shares[1], gates[3][0]])
    share(3, [shares[2], came[1]])
    own = own_shares(
        jnp.stack([here]).astype(jnp.int32), weight, weight_other,
        list(zip(gates, others)), [shares[-1], came[-2]],
    )
    out = None
    for mine, far_share, (at, span) in zip(own, came, parts):
        out = finish_chunk(mine, far_share, out, at, span, seg_len)
    return out.reshape(tok, ch)


def solution(mesh):
    placed = (
        P("seq", "tp"),
        P("seq", "tp"),
        P("seq", "tp"),
        P(None, "tp"),
        P(None, "tp"),
        P("tp"),
        P("tp", None),
    )
    return jax.shard_map(
        functools.partial(on_device, (4, 4, 4)),
        mesh=mesh,
        in_specs=placed,
        out_specs=P("seq", "tp"),
        check_vma=False,
    )
```

```python
import functools

import jax
import jax.numpy as jnp
from jax import lax
from jax.experimental import pallas as pl
from jax.experimental.pallas import tpu as pltpu
from jax.sharding import PartitionSpec as P

SEG = 8
LANES = 128
SPANS = (32, 32, 32, 32)
PIECE = 128
VMEM_LIMIT = 32 * 2**20
SIBLING = [(0, 1), (1, 0), (2, 3), (3, 2)]
PARTNER = [(0, 2), (2, 0), (1, 3), (3, 1)]
ANY = pl.BlockSpec(memory_space=pl.ANY)


def cost(flops, moved):
    return pl.CostEstimate(flops=1, bytes_accessed=1, transcendentals=0)


def spread(table):
    return [jnp.broadcast_to(table[n : n + 1], (SEG, LANES)) for n in range(table.shape[0])]


def end_kernel(seg_len, k_ref, v_ref, lam_ref, last_ref, before_ref, sent_ref, x_ref):
    order = lam_ref.shape[0]
    pitch = seg_len + 1
    for group in range(k_ref.shape[1] // LANES):
        cols = slice(group * LANES, (group + 1) * LANES)
        for seg in range(SEG):
            rows = pl.ds(seg * seg_len, seg_len)
            x = k_ref[rows, cols].astype(jnp.float32) * v_ref[rows, cols].astype(jnp.float32)
            x_ref[pl.ds(seg * pitch, seg_len), :] = x
        lam = lam_ref[:, cols]
        decay = spread(jnp.exp(-lam))

        def body(it, state):
            for u in range(16):
                x = x_ref[pl.ds(it * 16 + u, SEG, stride=pitch), :]
                state = tuple(h * d + x for h, d in zip(state, decay))
            return state

        zero = jnp.zeros((SEG, LANES), jnp.float32)
        state = lax.fori_loop(0, seg_len // 16, body, (zero,) * order)
        row = lax.broadcasted_iota(jnp.int32, (SEG, LANES), 0)
        hops = {step: spread(jnp.exp(lam * (-float(seg_len * step)))) for step in (1, 2, 4)}
        for n in range(order):
            run = state[n]
            for step, hop in hops.items():
                run = run + jnp.where(row >= step, hop[n] * pltpu.roll(run, step, 0), 0.0)
            last_ref[n : n + 1, cols] = run[SEG - 1 : SEG]
            sent_ref[n : n + 1, cols] = run[SEG - 1 : SEG].astype(jnp.bfloat16)
            before_ref[n * SEG : (n + 1) * SEG, cols] = jnp.where(
                row >= 1, pltpu.roll(run, 1, 0), 0.0
            )


def end_states(key, value, rates, width=256):
    tok, ch = key.shape
    order = rates.shape[0]
    seg_len = tok // SEG
    cut = lambda rows: pl.BlockSpec((rows, width), lambda j: (0, j))
    return pl.pallas_call(
        functools.partial(end_kernel, seg_len),
        grid=(ch // width,),
        in_specs=[cut(tok), cut(tok), cut(order)],
        out_specs=[cut(order), cut(order * SEG), cut(order)],
        out_shape=[
            jax.ShapeDtypeStruct((order, ch), jnp.float32),
            jax.ShapeDtypeStruct((order * SEG, ch), jnp.float32),
            jax.ShapeDtypeStruct((order, ch), jnp.bfloat16),
        ],
        scratch_shapes=[pltpu.VMEM((SEG * (seg_len + 1), LANES), jnp.float32)],
        compiler_params=pltpu.CompilerParams(vmem_limit_bytes=VMEM_LIMIT),
        cost_estimate=cost(2 * tok * ch * order, 4 * tok * ch),
        name="end_states",
    )(key, value, rates)


def gate_kernel(first, late, seg_len, q_ref, k_ref, v_ref, lam_ref, res_ref, skip_ref, state_ref, *rest):
    next_ref, x_ref, y_ref = rest[-3:]
    if first:
        inc_ref = rest[0]
    order = lam_ref.shape[0]
    span = q_ref.shape[1]
    held = PIECE // span
    g_refs = rest[-3 - SEG // held : -3]
    pitch = span + 1
    for group in range(q_ref.shape[2] // LANES):
        cols = slice(group * LANES, (group + 1) * LANES)
        lam = lam_ref[:, cols]
        decay = spread(jnp.exp(-lam))
        weight = spread(res_ref[:, cols] * jnp.sqrt(lam))
        state = [state_ref[n * SEG : (n + 1) * SEG, cols] for n in range(order)]
        if first:
            row = lax.broadcasted_iota(jnp.int32, (SEG, LANES), 0).astype(jnp.float32)
            reach = row * (-float(seg_len)) - float(late)
            state = [
                h + jnp.exp(lam[n : n + 1] * reach) * inc_ref[n : n + 1, cols]
                for n, h in enumerate(state)
            ]

        skip = skip_ref[:, cols]
        for seg in range(SEG):
            x = k_ref[seg, :, cols].astype(jnp.float32) * v_ref[seg, :, cols].astype(jnp.float32)
            x_ref[pl.ds(seg * pitch, span), :] = x

        def body(it, state):
            for u in range(16):
                where = pl.ds(it * 16 + u, SEG, stride=pitch)
                x = x_ref[where, :]
                state = tuple(h * d + x for h, d in zip(state, decay))
                terms = [w * h for w, h in zip(weight, state)]
                while len(terms) > 1:
                    terms = [a + b for a, b in zip(terms[::2], terms[1::2])]
                y_ref[where, :] = terms[0] + skip * x
            return state

        if span == 16:
            state = body(0, tuple(state))
        else:
            state = lax.fori_loop(0, span // 16, body, tuple(state))
        for n in range(order):
            next_ref[n * SEG : (n + 1) * SEG, cols] = state[n]
        for seg in range(SEG):
            gate = q_ref[seg, :, cols].astype(jnp.float32) * y_ref[pl.ds(seg * pitch, span), :]
            g_refs[seg // held][seg % held, :, cols] = gate.astype(jnp.bfloat16)


def gate_chunk(
    query, key, value, rates, residues, skip, state, incoming, after, at, span, width=None
):
    seg, seg_len, ch = query.shape
    order = rates.shape[0]
    first = incoming is not None
    width = width or (512 if span <= 16 else 256)
    part = pl.BlockSpec((seg, span, width), lambda j: (0, at // span, j))
    cut = lambda rows: pl.BlockSpec((rows, width), lambda j: (0, j))
    operands = [query, key, value, rates, residues, skip, state]
    in_specs = [part, part, part, cut(order), cut(order), cut(1), cut(order * seg)]
    if first:
        operands.append(incoming)
        in_specs.append(cut(order))
    operands.extend(after)
    in_specs.extend([ANY] * len(after))
    rows = seg * span
    held = PIECE // span
    count = seg // held
    *gated, state = pl.pallas_call(
        functools.partial(gate_kernel, first, at, seg_len),
        grid=(ch // width,),
        in_specs=in_specs,
        out_specs=[pl.BlockSpec((held, span, width), lambda j: (0, 0, j))] * count
        + [cut(order * seg)],
        out_shape=[jax.ShapeDtypeStruct((held, span, ch), jnp.bfloat16)] * count
        + [
            jax.ShapeDtypeStruct((order * seg, ch), jnp.float32),
        ],
        scratch_shapes=[pltpu.VMEM((seg * (span + 1), LANES), jnp.float32)] * 2,
        compiler_params=pltpu.CompilerParams(vmem_limit_bytes=VMEM_LIMIT),
        cost_estimate=cost(4 * rows * ch * order, 8 * rows * ch + 8 * order * seg * ch),
        name="gate_chunk",
    )(*operands)
    return [piece.reshape(PIECE, ch) for piece in gated], state


def columns_kernel(at_ref, w_ref, wo_ref, out_ref, mark_ref):
    depth = w_ref.shape[0]
    mark_ref[...] = jnp.zeros_like(mark_ref)
    out_ref[:depth] = w_ref[...]
    out_ref[depth:] = wo_ref[...]


def chip_columns(start, count, weight, weight_other, order, width=256):
    ch = weight.shape[0]
    part = pl.BlockSpec((ch, width), lambda j, at: (0, at[0] + j))
    return pl.pallas_call(
        columns_kernel,
        grid_spec=pltpu.PrefetchScalarGridSpec(
            num_scalar_prefetch=1,
            grid=(count // width,),
            in_specs=[part, part],
            out_specs=[
                pl.BlockSpec((2 * ch, width), lambda j, at: (0, j)),
                pl.BlockSpec((order, ch), lambda j, at: (0, 0)),
            ],
        ),
        out_shape=[
            pltpu.HBM((2 * ch, count), weight.dtype),
            jax.ShapeDtypeStruct((order, ch), jnp.float32),
        ],
        compiler_params=pltpu.CompilerParams(vmem_limit_bytes=VMEM_LIMIT),
        cost_estimate=cost(0, 8 * ch * count),
        name="chip_columns",
    )((start // width)[None].astype(jnp.int32), weight, weight_other)


def gathered(pieces):
    return jnp.concatenate([piece[...] for piece in pieces], axis=0)


def product(mine, other, weight, weight_other):
    total = jnp.dot(gathered(mine), weight, preferred_element_type=jnp.float32)
    return total + jnp.dot(gathered(other), weight_other, preferred_element_type=jnp.float32)


def share_kernel(count, w_ref, wx_ref, *rest):
    out_ref = rest[-1]
    depth = w_ref.shape[0] // 2
    width = w_ref.shape[1]
    for part, ref in enumerate((w_ref, wx_ref)):
        total = product(rest[:count], rest[count : 2 * count], ref[:depth], ref[depth:])
        out_ref[:, part * width : (part + 1) * width] = total.astype(out_ref.dtype)


def share_chunk(mine, other, weights, after):
    count = len(mine)
    depth, half = weights[0].shape
    rows, ch = count * PIECE, depth // 2
    whole = lambda *shape: pl.BlockSpec(shape, lambda: (0, 0))
    return pl.pallas_call(
        functools.partial(share_kernel, count),
        in_specs=[whole(depth, half)] * 2 + [whole(PIECE, ch)] * (2 * count) + [ANY] * len(after),
        out_specs=whole(rows, 2 * half),
        out_shape=jax.ShapeDtypeStruct((rows, 2 * half), jnp.bfloat16),
        compiler_params=pltpu.CompilerParams(vmem_limit_bytes=VMEM_LIMIT),
        cost_estimate=cost(4 * rows * ch * half, 4 * ch * half + 6 * rows * ch),
        name="share_chunk",
    )(*weights, *mine, *other, *after)


def own_kernel(counts, at_ref, w_ref, wo_ref, *rest):
    outs = rest[-len(counts) :]
    at = 0
    for count, out_ref in zip(counts, outs):
        out_ref[...] = product(
            rest[at : at + count], rest[at + count : at + 2 * count], w_ref[...], wo_ref[...]
        )
        at += 2 * count


def own_shares(block, weight, weight_other, pairs, after, width=256):
    ch = weight.shape[0]
    per = ch // width
    counts = [len(mine) for mine, _ in pairs]
    pieces = [piece for mine, other in pairs for piece in [*mine, *other]]
    rows = [count * PIECE for count in counts]
    columns = pl.BlockSpec((ch, width), lambda j, at: (0, at[0] * per + j))
    return pl.pallas_call(
        functools.partial(own_kernel, counts),
        grid_spec=pltpu.PrefetchScalarGridSpec(
            num_scalar_prefetch=1,
            grid=(per,),
            in_specs=[columns, columns]
            + [pl.BlockSpec((PIECE, ch), lambda j, at: (0, 0))] * len(pieces)
            + [ANY] * len(after),
            out_specs=[pl.BlockSpec((r, width), lambda j, at: (0, j)) for r in rows],
        ),
        out_shape=[jax.ShapeDtypeStruct((r, ch), jnp.float32) for r in rows],
        compiler_params=pltpu.CompilerParams(vmem_limit_bytes=VMEM_LIMIT),
        cost_estimate=cost(4 * sum(rows) * ch * ch, 4 * ch * ch + 8 * sum(rows) * ch),
        name="own_shares",
    )(block, weight, weight_other, *pieces, *after)


def finish_kernel(mine_ref, far_ref, *rest):
    out_ref = rest[-1]
    total = mine_ref[...] + far_ref[...].astype(jnp.float32)
    out_ref[...] = total.astype(out_ref.dtype).reshape(out_ref.shape)


def finish_chunk(mine, far, out, at, span, seg_len, width=512):
    rows, ch = mine.shape
    seg = rows // span
    cut = pl.BlockSpec((rows, width), lambda j: (0, j))
    operands, in_specs, aliases = [mine, far], [cut, cut], {}
    if out is not None:
        operands.append(out)
        in_specs.append(ANY)
        aliases = {2: 0}
    return pl.pallas_call(
        finish_kernel,
        grid=(ch // width,),
        in_specs=in_specs,
        out_specs=pl.BlockSpec((seg, span, width), lambda j: (0, at // span, j)),
        out_shape=jax.ShapeDtypeStruct((seg, seg_len, ch), jnp.bfloat16),
        input_output_aliases=aliases,
        compiler_params=pltpu.CompilerParams(vmem_limit_bytes=VMEM_LIMIT),
        cost_estimate=cost(rows * ch, 8 * rows * ch),
        name="finish_chunk",
    )(*operands)


def in_hbm(array):
    return pltpu.with_memory_space_constraint(array, pltpu.HBM)


def shifted(sizes, dim, hop, wrap):
    pairs = []
    total = 1
    for size in sizes:
        total *= size
    inner = 1
    for size in sizes[dim + 1 :]:
        inner *= size
    size = sizes[dim]
    for index in range(total):
        place = index // inner % size
        goal = place + hop
        if goal >= size and not wrap:
            continue
        pairs.append((index, index + (goal % size - place) * inner))
    return pairs


def carried_in(state, sent, rates, length, sizes, marks):
    mine = lax.axis_index("seq")
    fade = jnp.exp(rates * (-float(length)))
    levels = []
    for dim in reversed(range(len(sizes))):
        size = sizes[dim]
        place = mine % size
        mine = mine // size
        got = [
            lax.ppermute(sent, "seq", shifted(sizes, dim, hop, True))
            for hop in range(1, size)
        ]
        got = [part.astype(jnp.float32) for part in got]
        if dim in marks:
            got = [part + marks[dim] for part in got]
        powers = [jnp.ones_like(fade), fade]
        while len(powers) <= size:
            powers.append(powers[-1] * fade)

        def power(exponent):
            return sum(jnp.where(exponent == i, powers[i], 0.0) for i in range(size))

        prefix = sum(
            jnp.where(hop <= place, powers[hop - 1], 0.0) * part
            for hop, part in enumerate(got, 1)
        )
        levels.append((prefix, power(place)))
        if dim > 0:
            state = state * power(size - 1 - place) + sum(
                power(size - 1 - (place - hop) % size) * part for hop, part in enumerate(got, 1)
            )
            sent = state.astype(jnp.bfloat16)
        fade = powers[size]
    incoming = levels[-1][0]
    for prefix, drop in reversed(levels[:-1]):
        incoming = prefix + drop * incoming
    return incoming


def on_device(sizes, query, key, value, rates, residues, skip_gain, weight):
    tok, ch = query.shape
    seg_len = tok // SEG
    here = lax.axis_index("tp")
    chip, core = here // 2, here % 2
    weight_other = in_hbm(lax.ppermute(weight, "tp", SIBLING))
    weight = in_hbm(weight)
    last, before, sent = end_states(in_hbm(key), in_hbm(value), in_hbm(rates))
    half = ch // 2
    begin = (2 * (1 - chip) + core) * ch
    weight_far, marks = zip(
        *(
            chip_columns(begin + part * half, half, weight, weight_other, rates.shape[0])
            for part in range(2)
        )
    )
    incoming = carried_in(last, sent, rates, tok, sizes, {2: marks[0], 1: marks[1]})
    view = lambda part: part.reshape(SEG, seg_len, ch)
    query, key, value = (in_hbm(view(part)) for part in (query, key, value))
    state, extra = before, incoming
    at = 0
    parts, shares, came = [], [], []
    gates, others = [], []

    def gate(i, after):
        nonlocal state, extra, at
        gated, state = gate_chunk(
            query, key, value, rates, residues, skip_gain[None],
            state, extra, after, at, SPANS[i],
        )
        extra = None
        gates.append(gated)
        others.append([lax.ppermute(piece, "tp", SIBLING) for piece in gated])
        parts.append((at, SPANS[i]))
        at += SPANS[i]

    def share(i, after):
        shares.append(share_chunk(gates[i], others[i], weight_far, after))
        came.append(lax.ppermute(shares[-1], "tp", PARTNER))

    gate(0, [])
    share(0, [])
    gate(1, [shares[0]])
    share(1, [shares[0]])
    gate(2, [shares[1]])
    gate(3, [came[0]])
    share(2, [shares[1], gates[3][0]])
    share(3, [shares[2], came[1]])
    own = own_shares(
        jnp.stack([here]).astype(jnp.int32), weight, weight_other,
        list(zip(gates, others)), [shares[-1], came[-2]],
    )
    out = None
    for mine, far_share, (at, span) in zip(own, came, parts):
        out = finish_chunk(mine, far_share, out, at, span, seg_len)
    return out.reshape(tok, ch)


def solution(mesh):
    placed = (
        P("seq", "tp"),
        P("seq", "tp"),
        P("seq", "tp"),
        P(None, "tp"),
        P(None, "tp"),
        P("tp"),
        P("tp", None),
    )
    return jax.shard_map(
        functools.partial(on_device, (4, 4, 4)),
        mesh=mesh,
        in_specs=placed,
        out_specs=P("seq", "tp"),
        check_vma=False,
    )
```

```python
import functools

import jax
import jax.numpy as jnp
from jax import lax
from jax.experimental import pallas as pl
from jax.experimental.pallas import tpu as pltpu
from jax.sharding import PartitionSpec as P

SEG = 8
LANES = 128
SPANS = (32, 32, 32, 32)
PIECES = (2, 2, 2, 2)
VMEM_LIMIT = 32 * 2**20
SIBLING = [(0, 1), (1, 0), (2, 3), (3, 2)]
PARTNER = [(0, 2), (2, 0), (1, 3), (3, 1)]
ANY = pl.BlockSpec(memory_space=pl.ANY)


def cost(flops, moved):
    return pl.CostEstimate(flops=1, bytes_accessed=1, transcendentals=0)


def spread(table):
    return [jnp.broadcast_to(table[n : n + 1], (SEG, LANES)) for n in range(table.shape[0])]


def end_kernel(seg_len, k_ref, v_ref, lam_ref, last_ref, before_ref, sent_ref, x_ref):
    order = lam_ref.shape[0]
    pitch = seg_len + 1
    for group in range(k_ref.shape[1] // LANES):
        cols = slice(group * LANES, (group + 1) * LANES)
        for seg in range(SEG):
            rows = pl.ds(seg * seg_len, seg_len)
            x = k_ref[rows, cols].astype(jnp.float32) * v_ref[rows, cols].astype(jnp.float32)
            x_ref[pl.ds(seg * pitch, seg_len), :] = x
        lam = lam_ref[:, cols]
        decay = spread(jnp.exp(-lam))

        def body(it, state):
            for u in range(16):
                x = x_ref[pl.ds(it * 16 + u, SEG, stride=pitch), :]
                state = tuple(h * d + x for h, d in zip(state, decay))
            return state

        zero = jnp.zeros((SEG, LANES), jnp.float32)
        state = lax.fori_loop(0, seg_len // 16, body, (zero,) * order)
        row = lax.broadcasted_iota(jnp.int32, (SEG, LANES), 0)
        hops = {step: spread(jnp.exp(lam * (-float(seg_len * step)))) for step in (1, 2, 4)}
        for n in range(order):
            run = state[n]
            for step, hop in hops.items():
                run = run + jnp.where(row >= step, hop[n] * pltpu.roll(run, step, 0), 0.0)
            last_ref[n : n + 1, cols] = run[SEG - 1 : SEG]
            sent_ref[n : n + 1, cols] = run[SEG - 1 : SEG].astype(jnp.bfloat16)
            before_ref[n * SEG : (n + 1) * SEG, cols] = jnp.where(
                row >= 1, pltpu.roll(run, 1, 0), 0.0
            )


def end_states(key, value, rates, width=256):
    tok, ch = key.shape
    order = rates.shape[0]
    seg_len = tok // SEG
    cut = lambda rows: pl.BlockSpec((rows, width), lambda j: (0, j))
    return pl.pallas_call(
        functools.partial(end_kernel, seg_len),
        grid=(ch // width,),
        in_specs=[cut(tok), cut(tok), cut(order)],
        out_specs=[cut(order), cut(order * SEG), cut(order)],
        out_shape=[
            jax.ShapeDtypeStruct((order, ch), jnp.float32),
            jax.ShapeDtypeStruct((order * SEG, ch), jnp.float32),
            jax.ShapeDtypeStruct((order, ch), jnp.bfloat16),
        ],
        scratch_shapes=[pltpu.VMEM((SEG * (seg_len + 1), LANES), jnp.float32)],
        compiler_params=pltpu.CompilerParams(vmem_limit_bytes=VMEM_LIMIT),
        cost_estimate=cost(2 * tok * ch * order, 4 * tok * ch),
        name="end_states",
    )(key, value, rates)


def ahead_kernel(q_ref, k_ref, v_ref, after_ref, q_out, x_out, mark_ref, x_ref):
    span, pitch = q_ref.shape[1], q_ref.shape[1] + 1
    mark_ref[...] = jnp.zeros_like(mark_ref)
    q_out[...] = q_ref[...]
    for group in range(q_ref.shape[2] // LANES):
        cols = slice(group * LANES, (group + 1) * LANES)
        for seg in range(SEG):
            x = k_ref[seg, :, cols].astype(jnp.float32) * v_ref[seg, :, cols].astype(jnp.float32)
            x_ref[pl.ds(seg * pitch, span), :] = x
        for u in range(span):
            x_out[u * SEG : (u + 1) * SEG, cols] = x_ref[pl.ds(u, SEG, stride=pitch), :]


def ahead(query, key, value, after, span, order, width=512):
    seg, seg_len, ch = query.shape
    part = pl.BlockSpec((seg, span, width), lambda j: (0, 0, j))
    cut = lambda rows: pl.BlockSpec((rows, width), lambda j: (0, j))
    return pl.pallas_call(
        ahead_kernel,
        grid=(ch // width,),
        in_specs=[part, part, part, ANY],
        out_specs=[part, cut(seg * span), cut(order)],
        out_shape=[
            jax.ShapeDtypeStruct((seg, span, ch), query.dtype),
            jax.ShapeDtypeStruct((seg * span, ch), jnp.float32),
            jax.ShapeDtypeStruct((order, ch), jnp.float32),
        ],
        scratch_shapes=[pltpu.VMEM((seg * (span + 1), LANES), jnp.float32)],
        compiler_params=pltpu.CompilerParams(vmem_limit_bytes=VMEM_LIMIT),
        cost_estimate=cost(seg * span * ch, 12 * seg * span * ch),
        name="ahead",
    )(query, key, value, after)


def gate_kernel(first, count, late, seg_len, q_ref, *rest):
    next_ref, x_ref, y_ref = rest[-3:]
    if first:
        x_ref, lam_ref, res_ref, skip_ref, state_ref, inc_ref = rest[:6]
    else:
        k_ref, v_ref, lam_ref, res_ref, skip_ref, state_ref = rest[:6]
    order = lam_ref.shape[0]
    span = q_ref.shape[1]
    held = SEG // count
    g_refs = rest[-3 - count : -3]
    pitch = span + 1
    for group in range(q_ref.shape[2] // LANES):
        cols = slice(group * LANES, (group + 1) * LANES)
        lam = lam_ref[:, cols]
        decay = spread(jnp.exp(-lam))
        weight = spread(res_ref[:, cols] * jnp.sqrt(lam))
        state = [state_ref[n * SEG : (n + 1) * SEG, cols] for n in range(order)]
        if first:
            row = lax.broadcasted_iota(jnp.int32, (SEG, LANES), 0).astype(jnp.float32)
            reach = row * (-float(seg_len)) - float(late)
            state = [
                h + jnp.exp(lam[n : n + 1] * reach) * inc_ref[n : n + 1, cols]
                for n, h in enumerate(state)
            ]

        skip = skip_ref[:, cols]
        for seg in range(0 if first else SEG):
            x = k_ref[seg, :, cols].astype(jnp.float32) * v_ref[seg, :, cols].astype(jnp.float32)
            x_ref[pl.ds(seg * pitch, span), :] = x

        def body(it, state):
            for u in range(16):
                where = pl.ds(it * 16 + u, SEG, stride=pitch)
                if first:
                    x = x_ref[pl.ds(pl.multiple_of((it * 16 + u) * SEG, SEG), SEG), cols]
                else:
                    x = x_ref[where, :]
                state = tuple(h * d + x for h, d in zip(state, decay))
                terms = [w * h for w, h in zip(weight, state)]
                while len(terms) > 1:
                    terms = [a + b for a, b in zip(terms[::2], terms[1::2])]
                y_ref[where, :] = terms[0] + skip * x
            return state

        if span == 16:
            state = body(0, tuple(state))
        else:
            state = lax.fori_loop(0, span // 16, body, tuple(state))
        for n in range(order):
            next_ref[n * SEG : (n + 1) * SEG, cols] = state[n]
        for seg in range(SEG):
            gate = q_ref[seg, :, cols].astype(jnp.float32) * y_ref[pl.ds(seg * pitch, span), :]
            g_refs[seg // held][seg % held, :, cols] = gate.astype(jnp.bfloat16)


def gate_chunk(
    query, inputs, rates, residues, skip, state, incoming, after, at, span, count, seg_len
):
    seg, _, ch = query.shape
    order = rates.shape[0]
    first = incoming is not None
    width = 512 if first else 256
    part = pl.BlockSpec((seg, span, width), lambda j: (0, at // span, j))
    cut = lambda rows: pl.BlockSpec((rows, width), lambda j: (0, j))
    operands = [query, *inputs, rates, residues, skip, state]
    taken = [cut(seg * span)] if first else [part, part]
    in_specs = [part, *taken, cut(order), cut(order), cut(1), cut(order * seg)]
    if first:
        operands.append(incoming)
        in_specs.append(cut(order))
    operands.extend(after)
    in_specs.extend([ANY] * len(after))
    rows = seg * span
    held = seg // count
    *gated, state = pl.pallas_call(
        functools.partial(gate_kernel, first, count, at, seg_len),
        grid=(ch // width,),
        in_specs=in_specs,
        out_specs=[pl.BlockSpec((held, span, width), lambda j: (0, 0, j))] * count
        + [cut(order * seg)],
        out_shape=[jax.ShapeDtypeStruct((held, span, ch), jnp.bfloat16)] * count
        + [
            jax.ShapeDtypeStruct((order * seg, ch), jnp.float32),
        ],
        scratch_shapes=[pltpu.VMEM((seg * (span + 1), LANES), jnp.float32)] * 2,
        compiler_params=pltpu.CompilerParams(vmem_limit_bytes=VMEM_LIMIT),
        cost_estimate=cost(4 * rows * ch * order, 8 * rows * ch + 8 * order * seg * ch),
        name="gate_chunk",
    )(*operands)
    return [piece.reshape(held * span, ch) for piece in gated], state


def columns_kernel(at_ref, w_ref, wo_ref, out_ref, mark_ref):
    depth = w_ref.shape[0]
    mark_ref[...] = jnp.zeros_like(mark_ref)
    out_ref[:depth] = w_ref[...]
    out_ref[depth:] = wo_ref[...]


def chip_columns(start, count, weight, weight_other, order, pinned, width=256):
    ch = weight.shape[0]
    part = pl.BlockSpec((ch, width), lambda j, at: (0, at[0] + j))
    return pl.pallas_call(
        columns_kernel,
        grid_spec=pltpu.PrefetchScalarGridSpec(
            num_scalar_prefetch=1,
            grid=(count // width,),
            in_specs=[part, part],
            out_specs=[
                pl.BlockSpec((2 * ch, width), lambda j, at: (0, j)),
                pl.BlockSpec((order, ch), lambda j, at: (0, 0)),
            ],
        ),
        out_shape=[
            (pltpu.HBM if pinned else jax.ShapeDtypeStruct)((2 * ch, count), weight.dtype),
            jax.ShapeDtypeStruct((order, ch), jnp.float32),
        ],
        compiler_params=pltpu.CompilerParams(vmem_limit_bytes=VMEM_LIMIT),
        cost_estimate=cost(0, 8 * ch * count),
        name="chip_columns",
    )((start // width)[None].astype(jnp.int32), weight, weight_other)


def gathered(pieces):
    return jnp.concatenate([piece[...] for piece in pieces], axis=0)


def product(mine, other, weight, weight_other):
    total = jnp.dot(gathered(mine), weight, preferred_element_type=jnp.float32)
    return total + jnp.dot(gathered(other), weight_other, preferred_element_type=jnp.float32)


def share_kernel(count, w_ref, wx_ref, *rest):
    out_ref = rest[-1]
    depth = w_ref.shape[0] // 2
    width = w_ref.shape[1]
    for part, ref in enumerate((w_ref, wx_ref)):
        total = product(rest[:count], rest[count : 2 * count], ref[:depth], ref[depth:])
        out_ref[:, part * width : (part + 1) * width] = total.astype(out_ref.dtype)


def share_chunk(mine, other, weights, after):
    count = len(mine)
    depth, half = weights[0].shape
    ch = depth // 2
    rows = sum(piece.shape[0] for piece in mine)
    pieces = [*mine, *other]
    whole = lambda *shape: pl.BlockSpec(shape, lambda: (0, 0))
    return pl.pallas_call(
        functools.partial(share_kernel, count),
        in_specs=[whole(depth, half)] * 2 + [whole(*piece.shape) for piece in pieces] + [ANY] * len(after),
        out_specs=whole(rows, 2 * half),
        out_shape=jax.ShapeDtypeStruct((rows, 2 * half), jnp.bfloat16),
        compiler_params=pltpu.CompilerParams(vmem_limit_bytes=VMEM_LIMIT),
        cost_estimate=cost(4 * rows * ch * half, 4 * ch * half + 6 * rows * ch),
        name="share_chunk",
    )(*weights, *mine, *other, *after)


def own_kernel(counts, at_ref, w_ref, wo_ref, *rest):
    outs = rest[-len(counts) :]
    at = 0
    for count, out_ref in zip(counts, outs):
        out_ref[...] = product(
            rest[at : at + count], rest[at + count : at + 2 * count], w_ref[...], wo_ref[...]
        )
        at += 2 * count


def own_shares(block, weight, weight_other, pairs, after, width=256):
    ch = weight.shape[0]
    per = ch // width
    counts = [len(mine) for mine, _ in pairs]
    pieces = [piece for mine, other in pairs for piece in [*mine, *other]]
    rows = [sum(piece.shape[0] for piece in mine) for mine, _ in pairs]
    columns = pl.BlockSpec((ch, width), lambda j, at: (0, at[0] * per + j))
    return pl.pallas_call(
        functools.partial(own_kernel, counts),
        grid_spec=pltpu.PrefetchScalarGridSpec(
            num_scalar_prefetch=1,
            grid=(per,),
            in_specs=[columns, columns]
            + [pl.BlockSpec(piece.shape, lambda j, at: (0, 0)) for piece in pieces]
            + [ANY] * len(after),
            out_specs=[pl.BlockSpec((r, width), lambda j, at: (0, j)) for r in rows],
        ),
        out_shape=[jax.ShapeDtypeStruct((r, ch), jnp.float32) for r in rows],
        compiler_params=pltpu.CompilerParams(vmem_limit_bytes=VMEM_LIMIT),
        cost_estimate=cost(4 * sum(rows) * ch * ch, 4 * ch * ch + 8 * sum(rows) * ch),
        name="own_shares",
    )(block, weight, weight_other, *pieces, *after)


def finish_kernel(mine_ref, far_ref, *rest):
    out_ref = rest[-1]
    total = mine_ref[...] + far_ref[...].astype(jnp.float32)
    out_ref[...] = total.astype(out_ref.dtype).reshape(out_ref.shape)


def finish_chunk(mine, far, out, at, span, seg_len, width=512):
    rows, ch = mine.shape
    seg = rows // span
    cut = pl.BlockSpec((rows, width), lambda j: (0, j))
    operands, in_specs, aliases = [mine, far], [cut, cut], {}
    if out is not None:
        operands.append(out)
        in_specs.append(ANY)
        aliases = {2: 0}
    return pl.pallas_call(
        finish_kernel,
        grid=(ch // width,),
        in_specs=in_specs,
        out_specs=pl.BlockSpec((seg, span, width), lambda j: (0, at // span, j)),
        out_shape=jax.ShapeDtypeStruct((seg, seg_len, ch), jnp.bfloat16),
        input_output_aliases=aliases,
        compiler_params=pltpu.CompilerParams(vmem_limit_bytes=VMEM_LIMIT),
        cost_estimate=cost(rows * ch, 8 * rows * ch),
        name="finish_chunk",
    )(*operands)


def in_hbm(array):
    return pltpu.with_memory_space_constraint(array, pltpu.HBM)


def shifted(sizes, dim, hop, wrap):
    pairs = []
    total = 1
    for size in sizes:
        total *= size
    inner = 1
    for size in sizes[dim + 1 :]:
        inner *= size
    size = sizes[dim]
    for index in range(total):
        place = index // inner % size
        goal = place + hop
        if goal >= size and not wrap:
            continue
        pairs.append((index, index + (goal % size - place) * inner))
    return pairs


def carried_in(state, sent, rates, length, sizes, marks):
    mine = lax.axis_index("seq")
    fade = jnp.exp(rates * (-float(length)))
    levels = []
    for dim in reversed(range(len(sizes))):
        size = sizes[dim]
        place = mine % size
        mine = mine // size
        got = [
            lax.ppermute(sent, "seq", shifted(sizes, dim, hop, True))
            for hop in range(1, size)
        ]
        got = [part.astype(jnp.float32) for part in got]
        if dim in marks:
            got = [part + marks[dim] for part in got]
        powers = [jnp.ones_like(fade), fade]
        while len(powers) <= size:
            powers.append(powers[-1] * fade)

        def power(exponent):
            return sum(jnp.where(exponent == i, powers[i], 0.0) for i in range(size))

        prefix = sum(
            jnp.where(hop <= place, powers[hop - 1], 0.0) * part
            for hop, part in enumerate(got, 1)
        )
        levels.append((prefix, power(place)))
        if dim > 0:
            state = state * power(size - 1 - place) + sum(
                power(size - 1 - (place - hop) % size) * part for hop, part in enumerate(got, 1)
            )
            sent = state.astype(jnp.bfloat16)
        fade = powers[size]
    incoming = levels[-1][0]
    for prefix, drop in reversed(levels[:-1]):
        incoming = prefix + drop * incoming
    return incoming


def on_device(sizes, query, key, value, rates, residues, skip_gain, weight):
    tok, ch = query.shape
    seg_len = tok // SEG
    here = lax.axis_index("tp")
    chip, core = here // 2, here % 2
    weight_other = in_hbm(lax.ppermute(weight, "tp", SIBLING))
    weight = in_hbm(weight)
    last, before, sent = end_states(in_hbm(key), in_hbm(value), in_hbm(rates))
    half = ch // 2
    begin = (2 * (1 - chip) + core) * ch
    weight_far, marks = zip(
        *(
            chip_columns(
                begin + part * half, half, weight, weight_other, rates.shape[0], part == 0
            )
            for part in range(2)
        )
    )
    view = lambda part: part.reshape(SEG, seg_len, ch)
    query, key, value = (in_hbm(view(part)) for part in (query, key, value))
    query_ahead, steps, mark = ahead(query, key, value, sent, SPANS[0], rates.shape[0])
    marks = {2: mark, 1: marks[0], 0: marks[1]}
    incoming = carried_in(last, sent, rates, tok, sizes, marks)
    state, extra = before, incoming
    at = 0
    parts, shares, came = [], [], []
    gates, others = [], []

    def gate(i, after):
        nonlocal state, extra, at
        first = [query_ahead, [steps]]
        gated, state = gate_chunk(
            *([query, [key, value]] if i else first), rates, residues, skip_gain[None],
            state, extra, after, at, SPANS[i], PIECES[i], seg_len,
        )
        extra = None
        gates.append(gated)
        others.append([lax.ppermute(piece, "tp", SIBLING) for piece in gated])
        parts.append((at, SPANS[i]))
        at += SPANS[i]

    def share(i, after):
        shares.append(share_chunk(gates[i], others[i], weight_far, after))
        came.append(lax.ppermute(shares[-1], "tp", PARTNER))

    gate(0, [])
    share(0, [])
    gate(1, [shares[0]])
    share(1, [shares[0]])
    gate(2, [shares[1]])
    gate(3, [came[0]])
    share(2, [shares[1], gates[3][0]])
    share(3, [shares[2], came[1]])
    own = own_shares(
        jnp.stack([here]).astype(jnp.int32), weight, weight_other,
        list(zip(gates, others)), [shares[-1], came[-2]],
    )
    out = None
    for mine, far_share, (at, span) in zip(own, came, parts):
        out = finish_chunk(mine, far_share, out, at, span, seg_len)
    return out.reshape(tok, ch)


def solution(mesh):
    placed = (
        P("seq", "tp"),
        P("seq", "tp"),
        P("seq", "tp"),
        P(None, "tp"),
        P(None, "tp"),
        P("tp"),
        P("tp", None),
    )
    return jax.shard_map(
        functools.partial(on_device, (4, 4, 4)),
        mesh=mesh,
        in_specs=placed,
        out_specs=P("seq", "tp"),
        check_vma=False,
    )
```

```python
import functools

import jax
import jax.numpy as jnp
from jax import lax
from jax.experimental import pallas as pl
from jax.experimental.pallas import tpu as pltpu
from jax.sharding import PartitionSpec as P

SEG = 8
LANES = 128
SPANS = (32, 32, 32, 32)
PIECES = (2, 2, 2, 2)
VMEM_LIMIT = 32 * 2**20
SIBLING = [(0, 1), (1, 0), (2, 3), (3, 2)]
PARTNER = [(0, 2), (2, 0), (1, 3), (3, 1)]
ANY = pl.BlockSpec(memory_space=pl.ANY)


def cost(flops, moved):
    return pl.CostEstimate(flops=1, bytes_accessed=1, transcendentals=0)


def spread(table):
    return [jnp.broadcast_to(table[n : n + 1], (SEG, LANES)) for n in range(table.shape[0])]


def end_kernel(seg_len, k_ref, v_ref, lam_ref, last_ref, before_ref, sent_ref, x_ref):
    order = lam_ref.shape[0]
    pitch = seg_len + 1
    for group in range(k_ref.shape[1] // LANES):
        cols = slice(group * LANES, (group + 1) * LANES)
        for seg in range(SEG):
            rows = pl.ds(seg * seg_len, seg_len)
            x = k_ref[rows, cols].astype(jnp.float32) * v_ref[rows, cols].astype(jnp.float32)
            x_ref[pl.ds(seg * pitch, seg_len), :] = x
        lam = lam_ref[:, cols]
        decay = spread(jnp.exp(-lam))

        def body(it, state):
            for u in range(16):
                x = x_ref[pl.ds(it * 16 + u, SEG, stride=pitch), :]
                state = tuple(h * d + x for h, d in zip(state, decay))
            return state

        zero = jnp.zeros((SEG, LANES), jnp.float32)
        state = lax.fori_loop(0, seg_len // 16, body, (zero,) * order)
        row = lax.broadcasted_iota(jnp.int32, (SEG, LANES), 0)
        hops = {step: spread(jnp.exp(lam * (-float(seg_len * step)))) for step in (1, 2, 4)}
        for n in range(order):
            run = state[n]
            for step, hop in hops.items():
                run = run + jnp.where(row >= step, hop[n] * pltpu.roll(run, step, 0), 0.0)
            last_ref[n : n + 1, cols] = run[SEG - 1 : SEG]
            before_ref[n * SEG : (n + 1) * SEG, cols] = jnp.where(
                row >= 1, pltpu.roll(run, 1, 0), 0.0
            )
        sent_ref[:, cols] = last_ref[:, cols].astype(jnp.bfloat16)


def end_states(key, value, rates, width=256):
    tok, ch = key.shape
    order = rates.shape[0]
    seg_len = tok // SEG
    cut = lambda rows: pl.BlockSpec((rows, width), lambda j: (0, j))
    return pl.pallas_call(
        functools.partial(end_kernel, seg_len),
        grid=(ch // width,),
        in_specs=[cut(tok), cut(tok), cut(order)],
        out_specs=[cut(order), cut(order * SEG), cut(order)],
        out_shape=[
            jax.ShapeDtypeStruct((order, ch), jnp.float32),
            jax.ShapeDtypeStruct((order * SEG, ch), jnp.float32),
            jax.ShapeDtypeStruct((order, ch), jnp.bfloat16),
        ],
        scratch_shapes=[pltpu.VMEM(((SEG + 1) * (seg_len + 1), LANES), jnp.float32)],
        compiler_params=pltpu.CompilerParams(vmem_limit_bytes=VMEM_LIMIT),
        cost_estimate=cost(2 * tok * ch * order, 4 * tok * ch),
        name="end_states",
    )(key, value, rates)


def ahead_kernel(q_ref, k_ref, v_ref, after_ref, q_out, x_out, mark_ref, x_ref):
    span, pitch = q_ref.shape[1], q_ref.shape[1] + 1
    mark_ref[...] = jnp.zeros_like(mark_ref)
    q_out[...] = q_ref[...]
    for group in range(q_ref.shape[2] // LANES):
        cols = slice(group * LANES, (group + 1) * LANES)
        for seg in range(SEG):
            x = k_ref[seg, :, cols].astype(jnp.float32) * v_ref[seg, :, cols].astype(jnp.float32)
            x_ref[pl.ds(seg * pitch, span), :] = x
        for u in range(span):
            x_out[u * SEG : (u + 1) * SEG, cols] = x_ref[pl.ds(u, SEG, stride=pitch), :]


def ahead(query, key, value, after, span, order, width=512):
    seg, seg_len, ch = query.shape
    part = pl.BlockSpec((seg, span, width), lambda j: (0, 0, j))
    cut = lambda rows: pl.BlockSpec((rows, width), lambda j: (0, j))
    return pl.pallas_call(
        ahead_kernel,
        grid=(ch // width,),
        in_specs=[part, part, part, ANY],
        out_specs=[part, cut(seg * span), cut(order)],
        out_shape=[
            jax.ShapeDtypeStruct((seg, span, ch), query.dtype),
            jax.ShapeDtypeStruct((seg * span, ch), jnp.float32),
            jax.ShapeDtypeStruct((order, ch), jnp.float32),
        ],
        scratch_shapes=[pltpu.VMEM(((seg + 1) * (span + 1), LANES), jnp.float32)],
        compiler_params=pltpu.CompilerParams(vmem_limit_bytes=VMEM_LIMIT),
        cost_estimate=cost(seg * span * ch, 12 * seg * span * ch),
        name="ahead",
    )(query, key, value, after)


def gate_kernel(first, count, late, seg_len, q_ref, *rest):
    next_ref, x_ref, y_ref = rest[-3:]
    if first:
        x_ref, lam_ref, res_ref, skip_ref, state_ref, inc_ref = rest[:6]
    else:
        k_ref, v_ref, lam_ref, res_ref, skip_ref, state_ref = rest[:6]
    order = lam_ref.shape[0]
    span = q_ref.shape[1]
    held = SEG // count
    g_refs = rest[-3 - count : -3]
    pitch = span + 1
    for group in range(q_ref.shape[2] // LANES):
        cols = slice(group * LANES, (group + 1) * LANES)
        lam = lam_ref[:, cols]
        decay = spread(jnp.exp(-lam))
        weight = spread(res_ref[:, cols] * jnp.sqrt(lam))
        state = [state_ref[n * SEG : (n + 1) * SEG, cols] for n in range(order)]
        if first:
            row = lax.broadcasted_iota(jnp.int32, (SEG, LANES), 0).astype(jnp.float32)
            reach = row * (-float(seg_len)) - float(late)
            state = [
                h + jnp.exp(lam[n : n + 1] * reach) * inc_ref[n : n + 1, cols]
                for n, h in enumerate(state)
            ]

        skip = skip_ref[:, cols]
        for seg in range(0 if first else SEG):
            x = k_ref[seg, :, cols].astype(jnp.float32) * v_ref[seg, :, cols].astype(jnp.float32)
            x_ref[pl.ds(seg * pitch, span), :] = x

        def body(it, state):
            for u in range(16):
                where = pl.ds(it * 16 + u, SEG, stride=pitch)
                if first:
                    x = x_ref[pl.ds(pl.multiple_of((it * 16 + u) * SEG, SEG), SEG), cols]
                else:
                    x = x_ref[where, :]
                state = tuple(h * d + x for h, d in zip(state, decay))
                terms = [w * h for w, h in zip(weight, state)]
                while len(terms) > 1:
                    terms = [a + b for a, b in zip(terms[::2], terms[1::2])]
                y_ref[where, :] = terms[0] + skip * x
            return state

        if span == 16:
            state = body(0, tuple(state))
        else:
            state = lax.fori_loop(0, span // 16, body, tuple(state))
        for n in range(order):
            next_ref[n * SEG : (n + 1) * SEG, cols] = state[n]
        for seg in range(SEG):
            gate = q_ref[seg, :, cols].astype(jnp.float32) * y_ref[pl.ds(seg * pitch, span), :]
            g_refs[seg // held][seg % held, :, cols] = gate.astype(jnp.bfloat16)


def gate_chunk(
    query, inputs, rates, residues, skip, state, incoming, after, at, span, count, seg_len
):
    seg, _, ch = query.shape
    order = rates.shape[0]
    first = incoming is not None
    width = ch if first else 256
    part = pl.BlockSpec((seg, span, width), lambda j: (0, at // span, j))
    cut = lambda rows: pl.BlockSpec((rows, width), lambda j: (0, j))
    operands = [query, *inputs, rates, residues, skip, state]
    taken = [cut(seg * span)] if first else [part, part]
    in_specs = [part, *taken, cut(order), cut(order), cut(1), cut(order * seg)]
    if first:
        operands.append(incoming)
        in_specs.append(cut(order))
    operands.extend(after)
    in_specs.extend([ANY] * len(after))
    rows = seg * span
    held = seg // count
    *gated, state = pl.pallas_call(
        functools.partial(gate_kernel, first, count, at, seg_len),
        grid=(ch // width,),
        in_specs=in_specs,
        out_specs=[pl.BlockSpec((held, span, width), lambda j: (0, 0, j))] * count
        + [cut(order * seg)],
        out_shape=[jax.ShapeDtypeStruct((held, span, ch), jnp.bfloat16)] * count
        + [
            jax.ShapeDtypeStruct((order * seg, ch), jnp.float32),
        ],
        scratch_shapes=[pltpu.VMEM(((seg + 1) * (span + 1), LANES), jnp.float32)] * 2,
        compiler_params=pltpu.CompilerParams(vmem_limit_bytes=VMEM_LIMIT),
        cost_estimate=cost(4 * rows * ch * order, 8 * rows * ch + 8 * order * seg * ch),
        name="gate_chunk",
    )(*operands)
    return [piece.reshape(held * span, ch) for piece in gated], state


def columns_kernel(at_ref, w_ref, wo_ref, out_ref, mark_ref):
    depth = w_ref.shape[0]
    mark_ref[...] = jnp.zeros_like(mark_ref)
    out_ref[:depth] = w_ref[...]
    out_ref[depth:] = wo_ref[...]


def chip_columns(start, count, weight, weight_other, order, pinned, width=256):
    ch = weight.shape[0]
    part = pl.BlockSpec((ch, width), lambda j, at: (0, at[0] + j))
    return pl.pallas_call(
        columns_kernel,
        grid_spec=pltpu.PrefetchScalarGridSpec(
            num_scalar_prefetch=1,
            grid=(count // width,),
            in_specs=[part, part],
            out_specs=[
                pl.BlockSpec((2 * ch, width), lambda j, at: (0, j)),
                pl.BlockSpec((order, ch), lambda j, at: (0, 0)),
            ],
        ),
        out_shape=[
            (pltpu.HBM if pinned else jax.ShapeDtypeStruct)((2 * ch, count), weight.dtype),
            jax.ShapeDtypeStruct((order, ch), jnp.float32),
        ],
        compiler_params=pltpu.CompilerParams(vmem_limit_bytes=VMEM_LIMIT),
        cost_estimate=cost(0, 8 * ch * count),
        name="chip_columns",
    )((start // width)[None].astype(jnp.int32), weight, weight_other)


def gathered(pieces):
    return jnp.concatenate([piece[...] for piece in pieces], axis=0)


def product(mine, other, weight, weight_other):
    total = jnp.dot(gathered(mine), weight, preferred_element_type=jnp.float32)
    return total + jnp.dot(gathered(other), weight_other, preferred_element_type=jnp.float32)


def share_kernel(count, w_ref, wx_ref, *rest):
    out_ref = rest[-1]
    depth = w_ref.shape[0] // 2
    width = w_ref.shape[1]
    for part, ref in enumerate((w_ref, wx_ref)):
        total = product(rest[:count], rest[count : 2 * count], ref[:depth], ref[depth:])
        out_ref[:, part * width : (part + 1) * width] = total.astype(out_ref.dtype)


def share_chunk(mine, other, weights, after):
    count = len(mine)
    depth, half = weights[0].shape
    ch = depth // 2
    rows = sum(piece.shape[0] for piece in mine)
    pieces = [*mine, *other]
    whole = lambda *shape: pl.BlockSpec(shape, lambda: (0, 0))
    return pl.pallas_call(
        functools.partial(share_kernel, count),
        in_specs=[whole(depth, half)] * 2 + [whole(*piece.shape) for piece in pieces] + [ANY] * len(after),
        out_specs=whole(rows, 2 * half),
        out_shape=jax.ShapeDtypeStruct((rows, 2 * half), jnp.bfloat16),
        compiler_params=pltpu.CompilerParams(vmem_limit_bytes=VMEM_LIMIT),
        cost_estimate=cost(4 * rows * ch * half, 4 * ch * half + 6 * rows * ch),
        name="share_chunk",
    )(*weights, *mine, *other, *after)


def own_kernel(counts, at_ref, w_ref, wo_ref, *rest):
    outs = rest[-len(counts) :]
    at = 0
    for count, out_ref in zip(counts, outs):
        out_ref[...] = product(
            rest[at : at + count], rest[at + count : at + 2 * count], w_ref[...], wo_ref[...]
        )
        at += 2 * count


def own_shares(block, weight, weight_other, pairs, after, width=256):
    ch = weight.shape[0]
    per = ch // width
    counts = [len(mine) for mine, _ in pairs]
    pieces = [piece for mine, other in pairs for piece in [*mine, *other]]
    rows = [sum(piece.shape[0] for piece in mine) for mine, _ in pairs]
    columns = pl.BlockSpec((ch, width), lambda j, at: (0, at[0] * per + j))
    return pl.pallas_call(
        functools.partial(own_kernel, counts),
        grid_spec=pltpu.PrefetchScalarGridSpec(
            num_scalar_prefetch=1,
            grid=(per,),
            in_specs=[columns, columns]
            + [pl.BlockSpec(piece.shape, lambda j, at: (0, 0)) for piece in pieces]
            + [ANY] * len(after),
            out_specs=[pl.BlockSpec((r, width), lambda j, at: (0, j)) for r in rows],
        ),
        out_shape=[jax.ShapeDtypeStruct((r, ch), jnp.float32) for r in rows],
        compiler_params=pltpu.CompilerParams(vmem_limit_bytes=VMEM_LIMIT),
        cost_estimate=cost(4 * sum(rows) * ch * ch, 4 * ch * ch + 8 * sum(rows) * ch),
        name="own_shares",
    )(block, weight, weight_other, *pieces, *after)


def finish_kernel(mine_ref, far_ref, *rest):
    out_ref = rest[-1]
    total = mine_ref[...] + far_ref[...].astype(jnp.float32)
    out_ref[...] = total.astype(out_ref.dtype).reshape(out_ref.shape)


def finish_chunk(mine, far, out, at, span, seg_len, width=512):
    rows, ch = mine.shape
    seg = rows // span
    cut = pl.BlockSpec((rows, width), lambda j: (0, j))
    operands, in_specs, aliases = [mine, far], [cut, cut], {}
    if out is not None:
        operands.append(out)
        in_specs.append(ANY)
        aliases = {2: 0}
    return pl.pallas_call(
        finish_kernel,
        grid=(ch // width,),
        in_specs=in_specs,
        out_specs=pl.BlockSpec((seg, span, width), lambda j: (0, at // span, j)),
        out_shape=jax.ShapeDtypeStruct((seg, seg_len, ch), jnp.bfloat16),
        input_output_aliases=aliases,
        compiler_params=pltpu.CompilerParams(vmem_limit_bytes=VMEM_LIMIT),
        cost_estimate=cost(rows * ch, 8 * rows * ch),
        name="finish_chunk",
    )(*operands)


def in_hbm(array):
    return pltpu.with_memory_space_constraint(array, pltpu.HBM)


def shifted(sizes, dim, hop, wrap):
    pairs = []
    total = 1
    for size in sizes:
        total *= size
    inner = 1
    for size in sizes[dim + 1 :]:
        inner *= size
    size = sizes[dim]
    for index in range(total):
        place = index // inner % size
        goal = place + hop
        if goal >= size and not wrap:
            continue
        pairs.append((index, index + (goal % size - place) * inner))
    return pairs


def carried_in(state, sent, rates, length, sizes, marks):
    mine = lax.axis_index("seq")
    fade = jnp.exp(rates * (-float(length)))
    levels = []
    for dim in reversed(range(len(sizes))):
        size = sizes[dim]
        place = mine % size
        mine = mine // size
        got = [
            lax.ppermute(sent, "seq", shifted(sizes, dim, hop, True))
            for hop in range(1, size)
        ]
        got = [part.astype(jnp.float32) for part in got]
        if dim in marks:
            got = [part + marks[dim] for part in got]
        powers = [jnp.ones_like(fade), fade]
        while len(powers) <= size:
            powers.append(powers[-1] * fade)

        def power(exponent):
            return sum(jnp.where(exponent == i, powers[i], 0.0) for i in range(size))

        prefix = sum(
            jnp.where(hop <= place, powers[hop - 1], 0.0) * part
            for hop, part in enumerate(got, 1)
        )
        levels.append((prefix, power(place)))
        if dim > 0:
            state = state * power(size - 1 - place) + sum(
                power(size - 1 - (place - hop) % size) * part for hop, part in enumerate(got, 1)
            )
            sent = state.astype(jnp.bfloat16)
        fade = powers[size]
    incoming = levels[-1][0]
    for prefix, drop in reversed(levels[:-1]):
        incoming = prefix + drop * incoming
    return incoming


def on_device(sizes, query, key, value, rates, residues, skip_gain, weight):
    tok, ch = query.shape
    seg_len = tok // SEG
    here = lax.axis_index("tp")
    chip, core = here // 2, here % 2
    weight_other = in_hbm(lax.ppermute(weight, "tp", SIBLING))
    weight = in_hbm(weight)
    last, before, sent = end_states(in_hbm(key), in_hbm(value), in_hbm(rates))
    half = ch // 2
    begin = (2 * (1 - chip) + core) * ch
    weight_far, marks = zip(
        *(
            chip_columns(
                begin + part * half, half, weight, weight_other, rates.shape[0], part == 0
            )
            for part in range(2)
        )
    )
    view = lambda part: part.reshape(SEG, seg_len, ch)
    query, key, value = (in_hbm(view(part)) for part in (query, key, value))
    query_ahead, steps, mark = ahead(query, key, value, sent, SPANS[0], rates.shape[0])
    marks = {2: mark, 1: marks[0], 0: marks[1]}
    incoming = carried_in(last, sent, rates, tok, sizes, marks)
    state, extra = before, incoming
    at = 0
    parts, shares, came = [], [], []
    gates, others = [], []

    def gate(i, after):
        nonlocal state, extra, at
        first = [query_ahead, [steps]]
        gated, state = gate_chunk(
            *([query, [key, value]] if i else first), rates, residues, skip_gain[None],
            state, extra, after, at, SPANS[i], PIECES[i], seg_len,
        )
        extra = None
        gates.append(gated)
        others.append([lax.ppermute(piece, "tp", SIBLING) for piece in gated])
        parts.append((at, SPANS[i]))
        at += SPANS[i]

    def share(i, after):
        shares.append(share_chunk(gates[i], others[i], weight_far, after))
        came.append(lax.ppermute(shares[-1], "tp", PARTNER))

    gate(0, [])
    share(0, [])
    gate(1, [shares[0]])
    share(1, [shares[0]])
    gate(2, [shares[1]])
    gate(3, [came[0]])
    share(2, [shares[1], gates[3][0]])
    share(3, [shares[2], came[1]])
    own = own_shares(
        jnp.stack([here]).astype(jnp.int32), weight, weight_other,
        list(zip(gates, others)), [shares[-1], came[-2]],
    )
    out = None
    for mine, far_share, (at, span) in zip(own, came, parts):
        out = finish_chunk(mine, far_share, out, at, span, seg_len)
    return out.reshape(tok, ch)


def solution(mesh):
    placed = (
        P("seq", "tp"),
        P("seq", "tp"),
        P("seq", "tp"),
        P(None, "tp"),
        P(None, "tp"),
        P("tp"),
        P("tp", None),
    )
    return jax.shard_map(
        functools.partial(on_device, (4, 4, 4)),
        mesh=mesh,
        in_specs=placed,
        out_specs=P("seq", "tp"),
        check_vma=False,
    )
```

```python
import functools

import jax
import jax.numpy as jnp
from jax import lax
from jax.experimental import pallas as pl
from jax.experimental.pallas import tpu as pltpu
from jax.sharding import PartitionSpec as P

SEG = 8
LANES = 128
SPANS = (32, 32, 32, 32)
PIECES = (2, 2, 2, 2)
VMEM_LIMIT = 32 * 2**20
SIBLING = [(0, 1), (1, 0), (2, 3), (3, 2)]
PARTNER = [(0, 2), (2, 0), (1, 3), (3, 1)]
ANY = pl.BlockSpec(memory_space=pl.ANY)


def cost(flops, moved):
    return pl.CostEstimate(flops=1, bytes_accessed=1, transcendentals=0)


def spread(table):
    return [jnp.broadcast_to(table[n : n + 1], (SEG, LANES)) for n in range(table.shape[0])]


def end_kernel(seg_len, k_ref, v_ref, lam_ref, last_ref, before_ref, sent_ref, x_ref):
    order = lam_ref.shape[0]
    pitch = seg_len + 1
    for group in range(k_ref.shape[1] // LANES):
        cols = slice(group * LANES, (group + 1) * LANES)
        for seg in range(SEG):
            rows = pl.ds(seg * seg_len, seg_len)
            x = k_ref[rows, cols].astype(jnp.float32) * v_ref[rows, cols].astype(jnp.float32)
            x_ref[pl.ds(seg * pitch, seg_len), :] = x
        lam = lam_ref[:, cols]
        decay = spread(jnp.exp(-lam))

        def body(it, state):
            for u in range(16):
                x = x_ref[pl.ds(it * 16 + u, SEG, stride=pitch), :]
                state = tuple(h * d + x for h, d in zip(state, decay))
            return state

        zero = jnp.zeros((SEG, LANES), jnp.float32)
        state = lax.fori_loop(0, seg_len // 16, body, (zero,) * order)
        row = lax.broadcasted_iota(jnp.int32, (SEG, LANES), 0)
        hops = {step: spread(jnp.exp(lam * (-float(seg_len * step)))) for step in (1, 2, 4)}
        for n in range(order):
            run = state[n]
            for step, hop in hops.items():
                run = run + jnp.where(row >= step, hop[n] * pltpu.roll(run, step, 0), 0.0)
            last_ref[n : n + 1, cols] = run[SEG - 1 : SEG]
            before_ref[n * SEG : (n + 1) * SEG, cols] = jnp.where(
                row >= 1, pltpu.roll(run, 1, 0), 0.0
            )
        sent_ref[:, cols] = last_ref[:, cols].astype(jnp.bfloat16)


def end_states(key, value, rates, width=256):
    tok, ch = key.shape
    order = rates.shape[0]
    seg_len = tok // SEG
    cut = lambda rows: pl.BlockSpec((rows, width), lambda j: (0, j))
    return pl.pallas_call(
        functools.partial(end_kernel, seg_len),
        grid=(ch // width,),
        in_specs=[cut(tok), cut(tok), cut(order)],
        out_specs=[cut(order), cut(order * SEG), cut(order)],
        out_shape=[
            jax.ShapeDtypeStruct((order, ch), jnp.float32),
            jax.ShapeDtypeStruct((order * SEG, ch), jnp.float32),
            jax.ShapeDtypeStruct((order, ch), jnp.bfloat16),
        ],
        scratch_shapes=[pltpu.VMEM(((SEG + 1) * (seg_len + 1), LANES), jnp.float32)],
        compiler_params=pltpu.CompilerParams(vmem_limit_bytes=VMEM_LIMIT),
        cost_estimate=cost(2 * tok * ch * order, 4 * tok * ch),
        name="end_states",
    )(key, value, rates)


def ahead_kernel(q_ref, k_ref, v_ref, after_ref, q_out, x_out, mark_ref, x_ref):
    span, pitch = q_ref.shape[1], q_ref.shape[1] + 1
    mark_ref[...] = jnp.zeros_like(mark_ref)
    q_out[...] = q_ref[...]
    for group in range(q_ref.shape[2] // LANES):
        cols = slice(group * LANES, (group + 1) * LANES)
        for seg in range(SEG):
            x = k_ref[seg, :, cols].astype(jnp.float32) * v_ref[seg, :, cols].astype(jnp.float32)
            x_ref[pl.ds(seg * pitch, span), :] = x
        for u in range(span):
            x_out[u * SEG : (u + 1) * SEG, cols] = x_ref[pl.ds(u, SEG, stride=pitch), :]


def ahead(query, key, value, after, span, order, width=512):
    seg, seg_len, ch = query.shape
    part = pl.BlockSpec((seg, span, width), lambda j: (0, 0, j))
    cut = lambda rows: pl.BlockSpec((rows, width), lambda j: (0, j))
    return pl.pallas_call(
        ahead_kernel,
        grid=(ch // width,),
        in_specs=[part, part, part, ANY],
        out_specs=[part, cut(seg * span), cut(order)],
        out_shape=[
            jax.ShapeDtypeStruct((seg, span, ch), query.dtype),
            jax.ShapeDtypeStruct((seg * span, ch), jnp.float32),
            jax.ShapeDtypeStruct((order, ch), jnp.float32),
        ],
        scratch_shapes=[pltpu.VMEM(((seg + 1) * (span + 1), LANES), jnp.float32)],
        compiler_params=pltpu.CompilerParams(vmem_limit_bytes=VMEM_LIMIT),
        cost_estimate=cost(seg * span * ch, 12 * seg * span * ch),
        name="ahead",
    )(query, key, value, after)


def gate_kernel(first, count, late, seg_len, q_ref, *rest):
    next_ref, x_ref, y_ref = rest[-3:]
    if first:
        x_ref, lam_ref, res_ref, skip_ref, state_ref, inc_ref = rest[:6]
    else:
        k_ref, v_ref, lam_ref, res_ref, skip_ref, state_ref = rest[:6]
    order = lam_ref.shape[0]
    span = q_ref.shape[1]
    held = SEG // count
    g_refs = rest[-3 - count : -3]
    pitch = span + 1
    for group in range(q_ref.shape[2] // LANES):
        cols = slice(group * LANES, (group + 1) * LANES)
        lam = lam_ref[:, cols]
        decay = spread(jnp.exp(-lam))
        weight = spread(res_ref[:, cols] * jnp.sqrt(lam))
        state = [state_ref[n * SEG : (n + 1) * SEG, cols] for n in range(order)]
        if first:
            row = lax.broadcasted_iota(jnp.int32, (SEG, LANES), 0).astype(jnp.float32)
            reach = row * (-float(seg_len)) - float(late)
            state = [
                h + jnp.exp(lam[n : n + 1] * reach) * inc_ref[n : n + 1, cols]
                for n, h in enumerate(state)
            ]

        skip = skip_ref[:, cols]
        for seg in range(0 if first else SEG):
            x = k_ref[seg, :, cols].astype(jnp.float32) * v_ref[seg, :, cols].astype(jnp.float32)
            x_ref[pl.ds(seg * pitch, span), :] = x

        def body(it, state):
            for u in range(16):
                where = pl.ds(it * 16 + u, SEG, stride=pitch)
                if first:
                    x = x_ref[pl.ds(pl.multiple_of((it * 16 + u) * SEG, SEG), SEG), cols]
                else:
                    x = x_ref[where, :]
                state = tuple(h * d + x for h, d in zip(state, decay))
                terms = [w * h for w, h in zip(weight, state)]
                while len(terms) > 1:
                    terms = [a + b for a, b in zip(terms[::2], terms[1::2])]
                y_ref[where, :] = terms[0] + skip * x
            return state

        if span == 16:
            state = body(0, tuple(state))
        else:
            state = lax.fori_loop(0, span // 16, body, tuple(state))
        for n in range(order):
            next_ref[n * SEG : (n + 1) * SEG, cols] = state[n]
        for seg in range(SEG):
            gate = q_ref[seg, :, cols].astype(jnp.float32) * y_ref[pl.ds(seg * pitch, span), :]
            g_refs[seg // held][seg % held, :, cols] = gate.astype(jnp.bfloat16)


def gate_chunk(
    query, inputs, rates, residues, skip, state, incoming, after, at, span, count, seg_len
):
    seg, _, ch = query.shape
    order = rates.shape[0]
    first = incoming is not None
    width = ch if first else 256
    part = pl.BlockSpec((seg, span, width), lambda j: (0, at // span, j))
    cut = lambda rows: pl.BlockSpec((rows, width), lambda j: (0, j))
    operands = [query, *inputs, rates, residues, skip, state]
    taken = [cut(seg * span)] if first else [part, part]
    in_specs = [part, *taken, cut(order), cut(order), cut(1), cut(order * seg)]
    if first:
        operands.append(incoming)
        in_specs.append(cut(order))
    operands.extend(after)
    in_specs.extend([ANY] * len(after))
    rows = seg * span
    held = seg // count
    *gated, state = pl.pallas_call(
        functools.partial(gate_kernel, first, count, at, seg_len),
        grid=(ch // width,),
        in_specs=in_specs,
        out_specs=[pl.BlockSpec((held, span, width), lambda j: (0, 0, j))] * count
        + [cut(order * seg)],
        out_shape=[jax.ShapeDtypeStruct((held, span, ch), jnp.bfloat16)] * count
        + [
            jax.ShapeDtypeStruct((order * seg, ch), jnp.float32),
        ],
        scratch_shapes=[pltpu.VMEM(((seg + 1) * (span + 1), LANES), jnp.float32)] * 2,
        compiler_params=pltpu.CompilerParams(vmem_limit_bytes=VMEM_LIMIT),
        cost_estimate=cost(4 * rows * ch * order, 8 * rows * ch + 8 * order * seg * ch),
        name="gate_chunk",
    )(*operands)
    return [piece.reshape(held * span, ch) for piece in gated], state


def columns_kernel(at_ref, w_ref, wo_ref, out_ref, mark_ref):
    depth = w_ref.shape[0]
    mark_ref[...] = jnp.zeros_like(mark_ref)
    out_ref[:depth] = w_ref[...]
    out_ref[depth:] = wo_ref[...]


def chip_columns(start, count, weight, weight_other, order, pinned, width=256):
    ch = weight.shape[0]
    part = pl.BlockSpec((ch, width), lambda j, at: (0, at[0] + j))
    return pl.pallas_call(
        columns_kernel,
        grid_spec=pltpu.PrefetchScalarGridSpec(
            num_scalar_prefetch=1,
            grid=(count // width,),
            in_specs=[part, part],
            out_specs=[
                pl.BlockSpec((2 * ch, width), lambda j, at: (0, j)),
                pl.BlockSpec((order, ch), lambda j, at: (0, 0)),
            ],
        ),
        out_shape=[
            (pltpu.HBM if pinned else jax.ShapeDtypeStruct)((2 * ch, count), weight.dtype),
            jax.ShapeDtypeStruct((order, ch), jnp.float32),
        ],
        compiler_params=pltpu.CompilerParams(vmem_limit_bytes=VMEM_LIMIT),
        cost_estimate=cost(0, 8 * ch * count),
        name="chip_columns",
    )((start // width)[None].astype(jnp.int32), weight, weight_other)


def gathered(pieces):
    return jnp.concatenate([piece[...] for piece in pieces], axis=0)


def product(mine, other, weight, weight_other):
    total = jnp.dot(gathered(mine), weight, preferred_element_type=jnp.float32)
    return total + jnp.dot(gathered(other), weight_other, preferred_element_type=jnp.float32)


def share_kernel(count, w_ref, wx_ref, *rest):
    out_ref = rest[-1]
    depth = w_ref.shape[0] // 2
    width = w_ref.shape[1]
    for part, ref in enumerate((w_ref, wx_ref)):
        total = product(rest[:count], rest[count : 2 * count], ref[:depth], ref[depth:])
        out_ref[:, part * width : (part + 1) * width] = total.astype(out_ref.dtype)


def share_chunk(mine, other, weights, after):
    count = len(mine)
    depth, half = weights[0].shape
    ch = depth // 2
    rows = sum(piece.shape[0] for piece in mine)
    pieces = [*mine, *other]
    whole = lambda *shape: pl.BlockSpec(shape, lambda: (0, 0))
    return pl.pallas_call(
        functools.partial(share_kernel, count),
        in_specs=[whole(depth, half)] * 2 + [whole(*piece.shape) for piece in pieces] + [ANY] * len(after),
        out_specs=whole(rows, 2 * half),
        out_shape=jax.ShapeDtypeStruct((rows, 2 * half), jnp.bfloat16),
        compiler_params=pltpu.CompilerParams(vmem_limit_bytes=VMEM_LIMIT),
        cost_estimate=cost(4 * rows * ch * half, 4 * ch * half + 6 * rows * ch),
        name="share_chunk",
    )(*weights, *mine, *other, *after)


def own_kernel(counts, at_ref, w_ref, wo_ref, *rest):
    outs = rest[-len(counts) :]
    at = 0
    for count, out_ref in zip(counts, outs):
        out_ref[...] = product(
            rest[at : at + count], rest[at + count : at + 2 * count], w_ref[...], wo_ref[...]
        )
        at += 2 * count


def own_shares(block, weight, weight_other, pairs, after, width=256):
    ch = weight.shape[0]
    per = ch // width
    counts = [len(mine) for mine, _ in pairs]
    pieces = [piece for mine, other in pairs for piece in [*mine, *other]]
    rows = [sum(piece.shape[0] for piece in mine) for mine, _ in pairs]
    columns = pl.BlockSpec((ch, width), lambda j, at: (0, at[0] * per + j))
    return pl.pallas_call(
        functools.partial(own_kernel, counts),
        grid_spec=pltpu.PrefetchScalarGridSpec(
            num_scalar_prefetch=1,
            grid=(per,),
            in_specs=[columns, columns]
            + [pl.BlockSpec(piece.shape, lambda j, at: (0, 0)) for piece in pieces]
            + [ANY] * len(after),
            out_specs=[pl.BlockSpec((r, width), lambda j, at: (0, j)) for r in rows],
        ),
        out_shape=[jax.ShapeDtypeStruct((r, ch), jnp.float32) for r in rows],
        compiler_params=pltpu.CompilerParams(vmem_limit_bytes=VMEM_LIMIT),
        cost_estimate=cost(4 * sum(rows) * ch * ch, 4 * ch * ch + 8 * sum(rows) * ch),
        name="own_shares",
    )(block, weight, weight_other, *pieces, *after)


def finish_kernel(mine_ref, far_ref, *rest):
    out_ref = rest[-1]
    total = mine_ref[...] + far_ref[...].astype(jnp.float32)
    out_ref[...] = total.astype(out_ref.dtype).reshape(out_ref.shape)


def finish_chunk(mine, far, out, at, span, seg_len, width=1024):
    rows, ch = mine.shape
    seg = rows // span
    cut = pl.BlockSpec((rows, width), lambda j: (0, j))
    operands, in_specs, aliases = [mine, far], [cut, cut], {}
    if out is not None:
        operands.append(out)
        in_specs.append(ANY)
        aliases = {2: 0}
    return pl.pallas_call(
        finish_kernel,
        grid=(ch // width,),
        in_specs=in_specs,
        out_specs=pl.BlockSpec((seg, span, width), lambda j: (0, at // span, j)),
        out_shape=jax.ShapeDtypeStruct((seg, seg_len, ch), jnp.bfloat16),
        input_output_aliases=aliases,
        compiler_params=pltpu.CompilerParams(vmem_limit_bytes=VMEM_LIMIT),
        cost_estimate=cost(rows * ch, 8 * rows * ch),
        name="finish_chunk",
    )(*operands)


def in_hbm(array):
    return pltpu.with_memory_space_constraint(array, pltpu.HBM)


def shifted(sizes, dim, hop, wrap):
    pairs = []
    total = 1
    for size in sizes:
        total *= size
    inner = 1
    for size in sizes[dim + 1 :]:
        inner *= size
    size = sizes[dim]
    for index in range(total):
        place = index // inner % size
        goal = place + hop
        if goal >= size and not wrap:
            continue
        pairs.append((index, index + (goal % size - place) * inner))
    return pairs


def carried_in(state, sent, rates, length, sizes, marks):
    mine = lax.axis_index("seq")
    fade = jnp.exp(rates * (-float(length)))
    levels = []
    for dim in reversed(range(len(sizes))):
        size = sizes[dim]
        place = mine % size
        mine = mine // size
        got = [
            lax.ppermute(sent, "seq", shifted(sizes, dim, hop, True))
            for hop in range(1, size)
        ]
        got = [part.astype(jnp.float32) for part in got]
        if dim in marks:
            got = [part + marks[dim] for part in got]
        powers = [jnp.ones_like(fade), fade]
        while len(powers) <= size:
            powers.append(powers[-1] * fade)

        def power(exponent):
            return sum(jnp.where(exponent == i, powers[i], 0.0) for i in range(size))

        prefix = sum(
            jnp.where(hop <= place, powers[hop - 1], 0.0) * part
            for hop, part in enumerate(got, 1)
        )
        levels.append((prefix, power(place)))
        if dim > 0:
            state = state * power(size - 1 - place) + sum(
                power(size - 1 - (place - hop) % size) * part for hop, part in enumerate(got, 1)
            )
            sent = state.astype(jnp.bfloat16)
        fade = powers[size]
    incoming = levels[-1][0]
    for prefix, drop in reversed(levels[:-1]):
        incoming = prefix + drop * incoming
    return incoming


def on_device(sizes, query, key, value, rates, residues, skip_gain, weight):
    tok, ch = query.shape
    seg_len = tok // SEG
    here = lax.axis_index("tp")
    chip, core = here // 2, here % 2
    last, before, sent = end_states(in_hbm(key), in_hbm(value), in_hbm(rates))
    late_weight, sent = lax.optimization_barrier((weight, sent))
    weight_other = in_hbm(lax.ppermute(late_weight, "tp", SIBLING))
    weight = in_hbm(weight)
    half = ch // 2
    begin = (2 * (1 - chip) + core) * ch
    weight_far, marks = zip(
        *(
            chip_columns(
                begin + part * half, half, weight, weight_other, rates.shape[0], part == 0
            )
            for part in range(2)
        )
    )
    view = lambda part: part.reshape(SEG, seg_len, ch)
    query, key, value = (in_hbm(view(part)) for part in (query, key, value))
    query_ahead, steps, mark = ahead(query, key, value, sent, SPANS[0], rates.shape[0])
    marks = {2: mark, 1: marks[0], 0: marks[1]}
    incoming = carried_in(last, sent, rates, tok, sizes, marks)
    state, extra = before, incoming
    at = 0
    parts, shares, came = [], [], []
    gates, others = [], []

    def gate(i, after):
        nonlocal state, extra, at
        first = [query_ahead, [steps]]
        gated, state = gate_chunk(
            *([query, [key, value]] if i else first), rates, residues, skip_gain[None],
            state, extra, after, at, SPANS[i], PIECES[i], seg_len,
        )
        extra = None
        gates.append(gated)
        others.append([lax.ppermute(piece, "tp", SIBLING) for piece in gated])
        parts.append((at, SPANS[i]))
        at += SPANS[i]

    def share(i, after):
        shares.append(share_chunk(gates[i], others[i], weight_far, after))
        came.append(lax.ppermute(shares[-1], "tp", PARTNER))

    gate(0, [])
    share(0, [])
    gate(1, [shares[0]])
    share(1, [shares[0]])
    gate(2, [shares[1]])
    gate(3, [came[0]])
    share(2, [shares[1], gates[3][0]])
    share(3, [shares[2], came[1]])
    own = own_shares(
        jnp.stack([here]).astype(jnp.int32), weight, weight_other,
        list(zip(gates, others)), [shares[-1], came[-2]],
    )
    out = None
    for mine, far_share, (at, span) in zip(own, came, parts):
        out = finish_chunk(mine, far_share, out, at, span, seg_len)
    return out.reshape(tok, ch)


def solution(mesh):
    placed = (
        P("seq", "tp"),
        P("seq", "tp"),
        P("seq", "tp"),
        P(None, "tp"),
        P(None, "tp"),
        P("tp"),
        P("tp", None),
    )
    return jax.shard_map(
        functools.partial(on_device, (4, 4, 4)),
        mesh=mesh,
        in_specs=placed,
        out_specs=P("seq", "tp"),
        check_vma=False,
    )
```
